256 devices in a mesh: ctx: 64 (over y, x, z_lo), tp: 4 (over z_hi, core).
Axes of the slice: x: 4, y: 4, z: 8 (z_hi: 2, z_lo: 4; z = z_hi * 4 + z_lo), core: 2. Of those that a mesh axis runs over, the one named last changes fastest.
Arguments:
- hidden_in: bfloat16 [131072, 1536], P('ctx', 'tp'), may hold values from -6 to 6
- fac_inner: bfloat16 [512, 512], replicated, may hold values from -0.25 to 0.25
- fac_outer: bfloat16 [256, 256], replicated, may hold values from -0.375 to 0.375
- inv_outer: bfloat16 [256, 256], replicated, may hold values from -0.375 to 0.375
- inv_inner: bfloat16 [512, 512], replicated, may hold values from -0.25 to 0.25
- kernel_freq: bfloat16 [256, 512, 1536], P(None, 'ctx', 'tp'), may hold values from -6 to 6
- gate_blocks: bfloat16 [1536, 384], P('tp'), may hold values from -0.3125 to 0.3125
- mix_first: bfloat16 [1536, 384], P('tp'), may hold values from -0.3125 to 0.3125
- mix_second: bfloat16 [1536, 384], P('tp'), may hold values from -0.3125 to 0.3125
- upstream: bfloat16 [131072, 1536], P('ctx', 'tp'), may hold values from -6 to 6
Outputs:
- layer_out: bfloat16 [131072, 1536], P('ctx', 'tp')
- grad_input: bfloat16 [131072, 1536], P('ctx', 'tp')
- grad_kernel: float32 [256, 512, 1536], P(None, 'ctx', 'tp')
- grad_gate: float32 [1536, 384], P('tp', 'ctx')
- grad_first: float32 [1536, 384], P('tp', 'ctx')
- grad_second: float32 [1536, 384], P('tp', 'ctx')
The draws below stay inside these ranges and needn't reach their ends.
All inputs are finite; a program needn't handle non-finite values.
Results may differ from the reference program's by a relative error of at most 0.015.
Values may be sent and summed in bfloat16 or wider, within the bound.
No kernel may reach another device: no remote copies, remote signals or barrier semaphores. Data moves between devices by JAX's collectives and lax.ppermute only.
A program may use at most 128 MiB of HBM per device.

```python
import math
import jax
import jax.numpy as jnp
from jax import lax

SEQ = 131072
BLK_B = 512
C = 1536
NBLK = 4
BLK_A = 256
CB = 384


def level_of(rng, shape, shards, low, largest):
    loudness = 1.0
    for axis_at, blocks in shards:
        steps = jax.random.uniform(jax.random.fold_in(jax.random.fold_in(rng, 6), axis_at), (blocks,), jnp.float32, low / len(shards), largest / len(shards))
        loudness = loudness * jnp.repeat(jnp.exp(steps), shape[axis_at] // blocks).reshape((-1,) + (1,) * (len(shape) - 1 - axis_at))
    return loudness


def centred(key, dims, scale, most, pieces=(), kind=jnp.bfloat16):
    drawn = scale * jax.random.normal(key, dims, jnp.float32)
    if pieces:
        drawn = drawn * level_of(key, dims, pieces, -0.22, 0.18)
    return jnp.clip(drawn, -most, most).astype(kind)


def setup_inputs(seed: int = 0) -> dict:
    seeds = jax.random.split(jax.random.key(seed), 11)
    return {
        "hidden_in": centred(seeds[0], (SEQ, C), 1.0, 6.0, ((0, 64), (1, 4))),
        "fac_inner": centred(seeds[1], (BLK_B, BLK_B), BLK_B ** -0.5, 0.25),
        "fac_outer": centred(seeds[2], (BLK_A, BLK_A), BLK_A ** -0.5, 0.375),
        "inv_outer": centred(seeds[3], (BLK_A, BLK_A), BLK_A ** -0.5, 0.375),
        "inv_inner": centred(seeds[4], (BLK_B, BLK_B), BLK_B ** -0.5, 0.25),
        "kernel_freq": centred(seeds[5], (BLK_A, BLK_B, C), 1.0, 6.0, ((1, 64), (2, 4))),
        "gate_blocks": centred(seeds[6], (C, CB), CB ** -0.5, 0.3125, ((0, 4),)),
        "mix_first": centred(seeds[7], (C, CB), CB ** -0.5, 0.3125, ((0, 4),)),
        "mix_second": centred(seeds[8], (C, CB), CB ** -0.5, 0.3125, ((0, 4),)),
        "upstream": centred(seeds[9], (SEQ, C), 1.0, 6.0, ((0, 64), (1, 4))),
    }


def gelu_exact(values):
    return jax.nn.gelu(values, approximate=False)

def widen(values):
    return values.astype(jnp.float32)

def shuffle_forward(matrix):
    row_count = matrix.shape[0]
    return matrix.reshape(row_count, NBLK, CB).transpose(0, 2, 1).reshape(row_count, C)

def shuffle_inverse(matrix):
    row_count = matrix.shape[0]
    return matrix.reshape(row_count, CB, NBLK).transpose(0, 2, 1).reshape(row_count, C)

def split_groups(matrix):
    return matrix.reshape(matrix.shape[0], NBLK, CB).transpose(1, 0, 2)

def join_groups(stacked):
    return stacked.transpose(1, 0, 2).reshape(stacked.shape[1], C)

def token_contract(left, right):
    return lax.dot_general(left, right, (((0,), (0,)), ((), ())), preferred_element_type=jnp.float32)

def right_transposed(left, right):
    return lax.dot_general(left, right, (((1,), (1,)), ((), ())), preferred_element_type=jnp.float32)

def conv_forward(tokens_part, kernel_part, fac_inner, fac_outer, inv_outer, inv_inner):
    cube_input = widen(tokens_part.reshape(BLK_A, BLK_B, CB))
    row_mixed = jnp.einsum('abc,be->aec', cube_input, widen(fac_inner)).astype(jnp.bfloat16)
    spectrum = jnp.einsum('aec,af->fec', widen(row_mixed), widen(fac_outer))
    filtered = (spectrum * widen(kernel_part)).astype(jnp.bfloat16)
    back_mixed = jnp.einsum('fec,fg->gec', widen(filtered), widen(inv_outer)).astype(jnp.bfloat16)
    conv_flat = jnp.einsum('aec,eb->abc', widen(back_mixed), widen(inv_inner)).reshape(SEQ, CB)
    return (spectrum, conv_flat)

def reference(hidden_in, fac_inner, fac_outer, inv_outer, inv_inner, kernel_freq, gate_blocks, mix_first, mix_second, upstream):
    kernel_groups = kernel_freq.reshape(BLK_A, BLK_B, NBLK, CB).transpose(2, 0, 1, 3)
    gate_groups = gate_blocks.reshape(NBLK, CB, CB)
    first_groups = mix_first.reshape(NBLK, CB, CB)
    second_groups = mix_second.reshape(NBLK, CB, CB)
    input_groups = split_groups(hidden_in)
    upstream_groups = split_groups(upstream)

    def front_group(operands):
        tokens_part, kernel_part, gate_part, first_part = operands
        spectrum, conv_flat = conv_forward(tokens_part, kernel_part, fac_inner, fac_outer, inv_outer, inv_inner)
        gate_open = jax.nn.sigmoid(jnp.dot(tokens_part, gate_part, preferred_element_type=jnp.float32))
        mixed = (widen(tokens_part) + gate_open * conv_flat).astype(jnp.bfloat16)
        first_out = jnp.dot(mixed, first_part, preferred_element_type=jnp.float32).astype(jnp.bfloat16)
        return (mixed, first_out)
    mixed_groups, first_outs = lax.map(front_group, (input_groups, kernel_groups, gate_groups, first_groups))
    shuffled = split_groups(shuffle_forward(join_groups(first_outs)))

    def second_group(operands):
        return jnp.dot(operands[0], operands[1], preferred_element_type=jnp.float32).astype(jnp.bfloat16)
    second_out = lax.map(second_group, (shuffled, second_groups))
    merged_wide = widen(shuffle_inverse(join_groups(second_out)))
    mixed_all = join_groups(mixed_groups)
    layer_out = (widen(mixed_all) + gelu_exact(merged_wide)).astype(jnp.bfloat16)
    unused, pull = jax.vjp(gelu_exact, merged_wide)
    grad_merged = pull(widen(upstream))[0].astype(jnp.bfloat16)
    grad_second_out = split_groups(shuffle_forward(grad_merged))

    def second_back(operands):
        shuffled_part, grad_part, second_part = operands
        grad_second = token_contract(shuffled_part, grad_part)
        grad_shuffled = right_transposed(grad_part, second_part).astype(jnp.bfloat16)
        return (grad_second, grad_shuffled)
    grad_seconds, grad_shuffled = lax.map(second_back, (shuffled, grad_second_out, second_groups))
    grad_first_out = split_groups(shuffle_inverse(join_groups(grad_shuffled)))

    def front_back(operands):
        tokens_part, kernel_part, gate_part, first_part, mixed_part, grad_part, upstream_part = operands
        spectrum, conv_flat = conv_forward(tokens_part, kernel_part, fac_inner, fac_outer, inv_outer, inv_inner)
        gate_open = jax.nn.sigmoid(jnp.dot(tokens_part, gate_part, preferred_element_type=jnp.float32))
        grad_first = token_contract(mixed_part, grad_part)
        grad_mixed = widen(upstream_part) + right_transposed(grad_part, first_part)
        grad_conv = (grad_mixed * gate_open).astype(jnp.bfloat16)
        grad_gate_pre = (grad_mixed * conv_flat * gate_open * (1.0 - gate_open)).astype(jnp.bfloat16)
        grad_gate = token_contract(tokens_part, grad_gate_pre)
        gate_back = right_transposed(grad_gate_pre, gate_part)
        grad_back = jnp.einsum('abc,eb->aec', widen(grad_conv.reshape(BLK_A, BLK_B, CB)), widen(inv_inner)).astype(jnp.bfloat16)
        grad_filtered = jnp.einsum('gec,fg->fec', widen(grad_back), widen(inv_outer))
        grad_kernel = grad_filtered * spectrum
        grad_spectrum = (grad_filtered * widen(kernel_part)).astype(jnp.bfloat16)
        grad_row = jnp.einsum('fec,af->aec', widen(grad_spectrum), widen(fac_outer)).astype(jnp.bfloat16)
        conv_back = jnp.einsum('aec,be->abc', widen(grad_row), widen(fac_inner)).reshape(SEQ, CB)
        grad_input = (grad_mixed + gate_back + conv_back).astype(jnp.bfloat16)
        return (grad_input, grad_kernel, grad_gate, grad_first)
    grad_inputs, grad_kernels, grad_gates, grad_firsts = lax.map(front_back, (input_groups, kernel_groups, gate_groups, first_groups, mixed_groups, grad_first_out, upstream_groups))
    loss_scale = 1.0 / math.sqrt(SEQ)
    grad_input = join_groups(grad_inputs)
    grad_kernel = grad_kernels.transpose(1, 2, 0, 3).reshape(BLK_A, BLK_B, C)
    return (layer_out, grad_input, grad_kernel, grad_gates.reshape(C, CB) * loss_scale, grad_firsts.reshape(C, CB) * loss_scale, grad_seconds.reshape(C, CB) * loss_scale)
```

```python
import math

import jax
import jax.numpy as jnp
from jax import lax
from jax.experimental import pallas as pl
from jax.experimental.pallas import tpu as pltpu
from jax.sharding import Mesh
from jax.sharding import PartitionSpec as P

CTX = ("y", "x", "z_lo")
TP = ("z_hi", "core")
HALVES = 2
BF = jnp.bfloat16
F32 = jnp.float32
TILE = 256
ROOT_HALF = math.sqrt(0.5)
INV_ROOT_2PI = 1.0 / math.sqrt(2.0 * math.pi)


def dot(left, right, dims=((1,), (0,)), precision=None):
    return lax.dot_general(
        left, right, (dims, ((), ())), precision=precision, preferred_element_type=F32
    )


def call(body, outs, args, flops, scratch=()):
    moved = sum(a.size * a.dtype.itemsize for a in args)
    moved += sum(math.prod(s) * jnp.dtype(d).itemsize for s, d in outs)
    return pl.pallas_call(
        body,
        out_shape=[jax.ShapeDtypeStruct(s, d) for s, d in outs],
        in_specs=[pl.BlockSpec(memory_space=pltpu.VMEM)] * len(args),
        out_specs=[pl.BlockSpec(memory_space=pltpu.VMEM)] * len(outs),
        scratch_shapes=list(scratch),
        compiler_params=pltpu.CompilerParams(vmem_limit_bytes=48 * 1024 * 1024),
        cost_estimate=pl.CostEstimate(
            flops=int(flops), bytes_accessed=int(moved), transcendentals=0
        ),
    )(*args)


def interleave(parts):
    n, w = parts[0].shape
    cut = [p.reshape(n // 8, 1, 8, w) for p in parts]
    return jnp.concatenate(cut, axis=1).reshape(2 * n, w).astype(BF)


def separate(both):
    n, w = both.shape
    cut = both.astype(F32).reshape(n // 16, 2, 8, w)
    return [cut[:, i].reshape(n // 2, w).astype(BF) for i in range(2)]


def inner_kernel(x_ref, mat_ref, out_ref):
    n = mat_ref.shape[0]
    for t in range(0, n, TILE):
        part = mat_ref[t : t + TILE, :]
        out_ref[2 * t : 2 * (t + TILE), :] = interleave(
            [dot(part, x_ref[i * n : (i + 1) * n, :]) for i in range(2)]
        )


def widen(got_ref, wide):
    for c in range(wide.shape[0]):
        wide[c] = got_ref[:, c * 128 : (c + 1) * 128].astype(F32)


def rows_of(wide, e):
    parts, n, _ = wide.shape
    return jnp.concatenate(
        [wide[c, pl.ds(e, n // 8, stride=8), :].astype(BF) for c in range(parts)], axis=1
    )


def regroup_kernel(got_ref, out_ref, wide):
    n, w = got_ref.shape
    widen(got_ref, wide)
    for e in range(8):
        out_ref[e] = rows_of(wide, e)


def spectral_kernel(first_ref, got_ref, a_ref, b_ref, freq_ref, spec_ref, *rest):
    forward = len(rest) == 5
    if forward:
        out0_ref, out1_ref, wide, back0, back1 = rest
    else:
        grad_ref, out0_ref, out1_ref, wide, back0, back1 = rest
    n, w = got_ref.shape
    m = n // 8
    widen(got_ref, wide)
    for e in range(8):
        last = rows_of(wide, e)
        values = dot(a_ref[:, :m], first_ref[e]) + dot(a_ref[:, m:], last)
        if forward:
            spec_ref[e] = values
        else:
            grad_ref[e] = values * spec_ref[e]
        filtered = (values * freq_ref[e].astype(F32)).astype(BF)
        result = dot(b_ref[...], filtered)
        for c in range(w // 128):
            back0[c, pl.ds(e, m, stride=8), :] = result[:m, c * 128 : (c + 1) * 128]
            back1[c, pl.ds(e, m, stride=8), :] = result[m:, c * 128 : (c + 1) * 128]
    for c in range(w // 128):
        out0_ref[:, c * 128 : (c + 1) * 128] = back0[c].astype(BF)
        out1_ref[:, c * 128 : (c + 1) * 128] = back1[c].astype(BF)


def front_kernel(got_ref, mat_ref, x_ref, gate_w_ref, first_t_ref,
                 conv_ref, gate_ref, mixed_ref, s0_ref, s1_ref, s2_ref, s3_ref):
    halves = separate(got_ref[...])
    n = mat_ref.shape[0]
    sends = (s0_ref, s1_ref, s2_ref, s3_ref)
    piece = s0_ref.shape[0]
    for i in range(2):
        for t in range(0, n, TILE):
            at = slice(i * n + t, i * n + t + TILE)
            conv = dot(mat_ref[t : t + TILE, :], halves[i])
            x = x_ref[at, :]
            gate = jax.nn.sigmoid(dot(x, gate_w_ref[...]))
            mixed = (x.astype(F32) + gate * conv).astype(BF)
            conv_ref[at, :] = conv
            gate_ref[at, :] = gate
            mixed_ref[at, :] = mixed
            first = dot(first_t_ref[...], mixed, ((1,), (1,))).astype(BF)
            for k in range(4):
                sends[k][:, at] = first[k * piece : (k + 1) * piece, :]


def middle_kernel(*refs):
    shuf, up = refs[:4], refs[4:8]
    w_ref, wt_ref = refs[8:10]
    all_ref, gso_ref = refs[10:12]
    merged, back = refs[12:16], refs[16:20]
    piece, n = shuf[0].shape
    for t in range(0, n, TILE):
        at = slice(t, t + TILE)
        xs = jnp.concatenate([r[:, at] for r in shuf], axis=0)
        ups = jnp.concatenate([r[:, at] for r in up], axis=0)
        all_ref[:, at] = xs
        out = dot(wt_ref[...], xs).astype(BF)
        m = out.astype(F32)
        slope = 0.5 * (1.0 + lax.erf(m * ROOT_HALF)) + m * (INV_ROOT_2PI * jnp.exp(-0.5 * m * m))
        gso = (ups.astype(F32) * slope).astype(BF)
        gso_ref[:, at] = gso
        gsh = dot(w_ref[...], gso).astype(BF)
        for k in range(4):
            merged[k][:, at] = out[k * piece : (k + 1) * piece, :]
            back[k][:, at] = gsh[k * piece : (k + 1) * piece, :]


def rear_kernel(g0_ref, g1_ref, g2_ref, g3_ref, first_t_ref, up_ref, gate_ref, conv_ref, mat_ref,
                out_ref, gm_ref, ggp_ref, gfo_ref, scratch):
    n = mat_ref.shape[0]
    for t in range(0, 2 * n, TILE):
        at = slice(t, t + TILE)
        gfo = jnp.concatenate([r[:, at] for r in (g0_ref, g1_ref, g2_ref, g3_ref)], axis=0)
        gfo_ref[:, at] = gfo
        gm = up_ref[at, :].astype(F32) + dot(gfo, first_t_ref[...], ((0,), (0,)))
        gate = gate_ref[at, :]
        opened = gm * gate
        scratch[at, :] = opened.astype(BF)
        gm_ref[at, :] = gm
        ggp_ref[at, :] = (opened * conv_ref[at, :] * (1.0 - gate)).astype(BF)
    for t in range(0, n, TILE):
        part = mat_ref[t : t + TILE, :]
        out_ref[2 * t : 2 * (t + TILE), :] = interleave(
            [dot(part, scratch[i * n : (i + 1) * n, :]) for i in range(2)]
        )


def last_kernel(got_ref, mat_ref, base_ref, out_ref):
    halves = separate(got_ref[...])
    n = mat_ref.shape[0]
    for i in range(2):
        for t in range(0, n, TILE):
            at = slice(i * n + t, i * n + t + TILE)
            out_ref[at, :] = (base_ref[at, :] + dot(mat_ref[t : t + TILE, :], halves[i])).astype(BF)


def swap(x):
    return lax.all_to_all(x, CTX, 0, 0, tiled=True)


def exchange(blocks):
    return [blocks[0]] + [
        lax.ppermute(blocks[k], TP, [(i, i ^ k) for i in range(4)]) for k in (1, 2, 3)
    ]


def one_hot(rows, columns, match):
    r = lax.broadcasted_iota(jnp.int32, (rows, columns), 0)
    c = lax.broadcasted_iota(jnp.int32, (rows, columns), 1)
    return match(r, c)


def local(
    hidden_in, fac_inner, fac_outer, inv_outer, inv_inner,
    kernel_freq, gate_blocks, mix_first, mix_second, upstream,
):
    rows, width = hidden_in.shape
    inner, outer = fac_inner.shape[0], fac_outer.shape[0]
    ctx = outer // (rows // inner)
    piece = width // 4
    toks = rows // HALVES
    cols = width // ctx
    me = lax.axis_index(TP)
    pair = range(HALVES)

    fo = fac_outer.reshape(ctx, 2, 2, outer).transpose(1, 0, 2, 3).reshape(outer, outer)
    io = inv_outer.reshape(outer, ctx, 2, 2).transpose(0, 2, 1, 3).reshape(outer, outer)
    fac_inner_t, inv_inner_t = fac_inner.T, inv_inner.T
    freq = kernel_freq.transpose(1, 0, 2)
    to_plain = one_hot(width, width, lambda r, c: ((r // piece) ^ me) * piece + r % piece == c)
    to_block = one_hot(width, width, lambda r, c: (r % piece) * 4 + ((r // piece) ^ me) == c)
    plain, block = to_plain.astype(BF), to_block.astype(BF)
    first_t = dot(plain, mix_first, ((1,), (1,))).astype(BF)
    second = dot(dot(block, mix_second).astype(BF), block, ((1,), (1,))).astype(BF)
    second_t = second.T

    x = [hidden_in[i * toks : (i + 1) * toks] for i in pair]
    u = [upstream[i * toks : (i + 1) * toks] for i in pair]

    got = []
    for i in pair:
        sent, = call(inner_kernel, [((toks, width), BF)], (x[i], fac_inner_t), 2 * toks * width * inner)
        got.append(swap(sent))
    up = []
    for i in pair:
        turned = dot(plain, u[i], ((1,), (1,))).astype(BF)
        up.append(exchange([turned[k * piece : (k + 1) * piece] for k in range(4)]))

    half = outer // 2
    eb = 8
    wide = pltpu.VMEM((width // 128, toks, 128), F32)

    def regroup(a):
        return call(regroup_kernel, [((eb, half, width), BF)], (a,), 0, (wide,))[0]

    spec_flops = 2 * 2 * outer * outer * eb * width
    spectrum, *sent = call(
        spectral_kernel,
        [((eb, outer, width), F32), ((toks, width), BF), ((toks, width), BF)],
        (regroup(got[0]), got[1], fo.T, io.T, freq), spec_flops, (wide, wide, wide),
    )
    got = [swap(s) for s in sent]

    conv, gate, mixed, shuf = [], [], [], []
    for i in pair:
        c, g, m, *blocks = call(
            front_kernel,
            [((toks, width), F32), ((toks, width), F32), ((toks, width), BF)]
            + [((piece, toks), BF)] * 4,
            (got[i], inv_inner_t, x[i], gate_blocks, first_t),
            2 * toks * width * (inner + 2 * width),
        )
        conv.append(c), gate.append(g), mixed.append(m)
        shuf.append(exchange(blocks))

    outs, bases, got = [], [], []
    sums = [0.0, 0.0, 0.0]
    for i in pair:
        shuf_all, gso, *blocks = call(
            middle_kernel,
            [((width, toks), BF)] * 2 + [((piece, toks), BF)] * 8,
            (*shuf[i], *up[i], second, second_t), 2 * toks * width * 2 * width,
        )
        back = exchange(blocks[4:])
        merged = exchange(blocks[:4])
        sent, gm, ggp, gfo = call(
            rear_kernel,
            [((toks, width), BF), ((toks, width), F32), ((toks, width), BF), ((width, toks), BF)],
            (*back, first_t, u[i], gate[i], conv[i], inv_inner), 2 * toks * width * (inner + width),
            (pltpu.VMEM((toks, width), BF),),
        )
        got.append(swap(sent))
        merged = dot(jnp.concatenate(merged, 0), plain, ((0,), (0,)))
        outs.append((mixed[i].astype(F32) + jax.nn.gelu(merged, approximate=False)).astype(BF))
        bases.append(gm + dot(ggp, gate_blocks, ((1,), (1,))))
        sums[0] += dot(ggp, x[i], ((0,), (0,)))
        sums[1] += dot(gfo, mixed[i])
        sums[2] += dot(gso, shuf_all, ((1,), (1,)))

    exact = lax.Precision.HIGHEST
    source = one_hot(ctx * 8, width, lambda r, c: jnp.where(r % 8 < cols, r // 8 * cols + r % 8, -1) == c)
    scale = 1.0 / math.sqrt(rows * ctx)
    picks = [source.astype(F32) * scale, dot(source.astype(F32), plain.T.astype(F32)) * scale,
             dot(source.astype(F32), block.T.astype(F32)) * scale]
    right = dot(sums[2], block.astype(F32), precision=exact)
    parts = [dot(p, s, precision=exact).reshape(ctx, 8, width)
             for p, s in zip(picks, (sums[0], sums[1], right))]
    total = jnp.concatenate(parts, axis=1)
    for axis in CTX:
        total = lax.psum_scatter(total, axis, scatter_dimension=0, tiled=True)
    total = total.reshape(3, 8, width)[:, :cols]

    grad_kernel, *sent = call(
        spectral_kernel,
        [((eb, outer, width), F32), ((toks, width), BF), ((toks, width), BF)],
        (regroup(got[0]), got[1], io, fo, freq, spectrum), spec_flops, (wide, wide, wide),
    )
    gins = []
    for i in pair:
        gins += call(
            last_kernel, [((toks, width), BF)], (swap(sent[i]), fac_inner, bases[i]),
            2 * toks * width * inner,
        )
    return (
        jnp.concatenate(outs, 0), jnp.concatenate(gins, 0), grad_kernel.transpose(1, 0, 2),
        total[0].T, total[1].T, total[2].T,
    )


def solution(mesh):
    fine = Mesh(mesh.devices.reshape(4, 4, 4, 2, 2), CTX + TP)
    tok = P(CTX, TP)
    mat = P(TP, None)
    small = P(TP, CTX)
    freq = P(None, CTX, TP)
    return jax.shard_map(
        local,
        mesh=fine,
        in_specs=(tok, P(), P(), P(), P(), freq, mat, mat, mat, tok),
        out_specs=(tok, tok, freq, small, small, small),
        check_vma=False,
    )
```

```python
import math

import jax
import jax.numpy as jnp
from jax import lax
from jax.experimental import pallas as pl
from jax.experimental.pallas import tpu as pltpu
from jax.sharding import Mesh
from jax.sharding import PartitionSpec as P

CTX = ("y", "x", "z_lo")
TP = ("z_hi", "core")
HALVES = 2
BF = jnp.bfloat16
F32 = jnp.float32
TILE = 256
ROOT_HALF = math.sqrt(0.5)
INV_ROOT_2PI = 1.0 / math.sqrt(2.0 * math.pi)


def dot(left, right, dims=((1,), (0,)), precision=None):
    return lax.dot_general(
        left, right, (dims, ((), ())), precision=precision, preferred_element_type=F32
    )


def call(body, outs, args, flops, scratch=(), after=()):
    arrays = [a[0] if isinstance(a, tuple) else a for a in args]
    specs = []
    for a in args:
        if isinstance(a, tuple):
            rows, width = a[0].shape
            specs.append(pl.BlockSpec((rows // HALVES, width), lambda g, i=a[1]: (i, 0)))
        else:
            specs.append(pl.BlockSpec(memory_space=pltpu.VMEM))
    halved = any(isinstance(a, tuple) for a in args)
    n, late = len(args), len(after)

    def wrapped(*refs):
        body(*refs[:n], *refs[n + late :])

    moved = sum(a.size * a.dtype.itemsize for a in arrays)
    moved += sum(math.prod(s) * jnp.dtype(d).itemsize for s, d in outs)
    return pl.pallas_call(
        wrapped,
        out_shape=[jax.ShapeDtypeStruct(s, d) for s, d in outs],
        in_specs=specs + [pl.BlockSpec(memory_space=pl.ANY)] * late,
        out_specs=[pl.BlockSpec(memory_space=pltpu.VMEM)] * len(outs),
        scratch_shapes=list(scratch),
        compiler_params=pltpu.CompilerParams(vmem_limit_bytes=48 * 1024 * 1024),
        cost_estimate=pl.CostEstimate(
            flops=int(flops), bytes_accessed=int(moved), transcendentals=0
        ),
        **({"grid": (1,)} if halved else {}),
    )(*arrays, *after)


def interleave(parts):
    n, w = parts[0].shape
    cut = [p.reshape(n // 8, 1, 8, w) for p in parts]
    return jnp.concatenate(cut, axis=1).reshape(2 * n, w).astype(BF)


def separate(both):
    n, w = both.shape
    cut = both.astype(F32).reshape(n // 16, 2, 8, w)
    return [cut[:, i].reshape(n // 2, w).astype(BF) for i in range(2)]


def inner_kernel(x_ref, mat_ref, out_ref):
    n = mat_ref.shape[0]
    for t in range(0, n, TILE):
        part = mat_ref[t : t + TILE, :]
        out_ref[2 * t : 2 * (t + TILE), :] = interleave(
            [dot(part, x_ref[i * n : (i + 1) * n, :]) for i in range(2)]
        )


def widen(got_ref, wide):
    for c in range(wide.shape[0]):
        wide[c] = got_ref[:, c * 128 : (c + 1) * 128].astype(F32)


def rows_of(wide, e):
    parts, n, _ = wide.shape
    return jnp.concatenate(
        [wide[c, pl.ds(e, n // 8, stride=8), :].astype(BF) for c in range(parts)], axis=1
    )


def regroup_kernel(got_ref, out_ref, wide):
    n, w = got_ref.shape
    widen(got_ref, wide)
    for e in range(8):
        out_ref[e] = rows_of(wide, e)


def spectral_kernel(first_ref, got_ref, a_ref, b_ref, freq_ref, spec_ref, *rest):
    forward = len(rest) == 5
    if forward:
        out0_ref, out1_ref, wide, back0, back1 = rest
    else:
        grad_ref, out0_ref, out1_ref, wide, back0, back1 = rest
    n, w = got_ref.shape
    m = n // 8
    widen(got_ref, wide)
    for e in range(8):
        last = rows_of(wide, e)
        values = dot(a_ref[:, :m], first_ref[e]) + dot(a_ref[:, m:], last)
        if forward:
            spec_ref[e] = values
        else:
            grad_ref[e] = values * spec_ref[e]
        filtered = (values * freq_ref[e].astype(F32)).astype(BF)
        result = dot(b_ref[...], filtered)
        for c in range(w // 128):
            back0[c, pl.ds(e, m, stride=8), :] = result[:m, c * 128 : (c + 1) * 128]
            back1[c, pl.ds(e, m, stride=8), :] = result[m:, c * 128 : (c + 1) * 128]
    for c in range(w // 128):
        out0_ref[:, c * 128 : (c + 1) * 128] = back0[c].astype(BF)
        out1_ref[:, c * 128 : (c + 1) * 128] = back1[c].astype(BF)


def front_kernel(got_ref, mat_ref, x_ref, gate_w_ref, first_t_ref,
                 conv_ref, gate_ref, mixed_ref, s0_ref, s1_ref, s2_ref, s3_ref):
    halves = separate(got_ref[...])
    n = mat_ref.shape[0]
    sends = (s0_ref, s1_ref, s2_ref, s3_ref)
    piece = s0_ref.shape[0]
    for i in range(2):
        for t in range(0, n, TILE):
            at = slice(i * n + t, i * n + t + TILE)
            conv = dot(mat_ref[t : t + TILE, :], halves[i])
            x = x_ref[at, :]
            gate = jax.nn.sigmoid(dot(x, gate_w_ref[...]))
            mixed = (x.astype(F32) + gate * conv).astype(BF)
            conv_ref[at, :] = conv
            gate_ref[at, :] = gate
            mixed_ref[at, :] = mixed
            first = dot(first_t_ref[...], mixed, ((1,), (1,))).astype(BF)
            for k in range(4):
                sends[k][:, at] = first[k * piece : (k + 1) * piece, :]


def middle_kernel(*refs):
    shuf, up = refs[:4], refs[4:8]
    w_ref, wt_ref = refs[8:10]
    all_ref, gso_ref = refs[10:12]
    merged, back = refs[12:16], refs[16:20]
    piece, n = shuf[0].shape
    for t in range(0, n, TILE):
        at = slice(t, t + TILE)
        xs = jnp.concatenate([r[:, at] for r in shuf], axis=0)
        ups = jnp.concatenate([r[:, at] for r in up], axis=0)
        all_ref[:, at] = xs
        out = dot(wt_ref[...], xs).astype(BF)
        m = out.astype(F32)
        slope = 0.5 * (1.0 + lax.erf(m * ROOT_HALF)) + m * (INV_ROOT_2PI * jnp.exp(-0.5 * m * m))
        gso = (ups.astype(F32) * slope).astype(BF)
        gso_ref[:, at] = gso
        gsh = dot(w_ref[...], gso).astype(BF)
        for k in range(4):
            merged[k][:, at] = out[k * piece : (k + 1) * piece, :]
            back[k][:, at] = gsh[k * piece : (k + 1) * piece, :]


def rear_kernel(g0_ref, g1_ref, g2_ref, g3_ref, first_t_ref, up_ref, gate_ref, conv_ref, mat_ref,
                out_ref, gm_ref, ggp_ref, gfo_ref, scratch):
    n = mat_ref.shape[0]
    for t in range(0, 2 * n, TILE):
        at = slice(t, t + TILE)
        gfo = jnp.concatenate([r[:, at] for r in (g0_ref, g1_ref, g2_ref, g3_ref)], axis=0)
        gfo_ref[:, at] = gfo
        gm = up_ref[at, :].astype(F32) + dot(gfo, first_t_ref[...], ((0,), (0,)))
        gate = gate_ref[at, :]
        opened = gm * gate
        scratch[at, :] = opened.astype(BF)
        gm_ref[at, :] = gm
        ggp_ref[at, :] = (opened * conv_ref[at, :] * (1.0 - gate)).astype(BF)
    for t in range(0, n, TILE):
        part = mat_ref[t : t + TILE, :]
        out_ref[2 * t : 2 * (t + TILE), :] = interleave(
            [dot(part, scratch[i * n : (i + 1) * n, :]) for i in range(2)]
        )


def last_kernel(got_ref, mat_ref, base_ref, out_ref):
    halves = separate(got_ref[...])
    n = mat_ref.shape[0]
    for i in range(2):
        for t in range(0, n, TILE):
            at = slice(i * n + t, i * n + t + TILE)
            out_ref[at, :] = (base_ref[at, :] + dot(mat_ref[t : t + TILE, :], halves[i])).astype(BF)


def turn_kernel(x_ref, plain_ref, *sends):
    piece, n = sends[0].shape
    for t in range(0, n, TILE):
        at = slice(t, t + TILE)
        turned = dot(plain_ref[...], x_ref[at, :], ((1,), (1,))).astype(BF)
        for k in range(4):
            sends[k][:, at] = turned[k * piece : (k + 1) * piece, :]


def prepare_kernel(order_ref, fo_ref, io_ref, plain_ref, block_ref, mix1_ref, mix2_ref,
                   fo_out, fo_t_out, io_out, io_t_out, first_t_out, second_out, second_t_out):
    order = order_ref[...]
    fo = dot(order, fo_ref[...])
    fo_out[...] = fo.astype(BF)
    fo_t_out[...] = fo.T.astype(BF)
    io = dot(io_ref[...], order, ((1,), (1,)))
    io_out[...] = io.astype(BF)
    io_t_out[...] = io.T.astype(BF)
    first_t_out[...] = dot(plain_ref[...], mix1_ref[...], ((1,), (1,))).astype(BF)
    block = block_ref[...]
    second = dot(dot(block, mix2_ref[...]).astype(BF), block, ((1,), (1,)))
    second_out[...] = second.astype(BF)
    second_t_out[...] = second.T.astype(BF)


def thirds(x):
    high = x.astype(BF)
    rest = x - high.astype(F32)
    middle = rest.astype(BF)
    return high, middle, (rest - middle.astype(F32)).astype(BF)


def pack_kernel(s0_ref, s1_ref, s2_ref, pick_ref, pick_plain_ref, pick_block_ref, block_ref, scale_ref,
                *outs):
    scale = scale_ref[0]
    s2 = sum(dot(p, block_ref[...]) for p in thirds(s2_ref[...]))
    cut = [thirds(s0_ref[...]), thirds(s1_ref[...]), thirds(s2)]
    w = s0_ref.shape[1]
    n = pick_ref.shape[0] // 4
    for k in range(4):
        parts = [
            (sum(dot(p[k * n : (k + 1) * n, :], x) for x in c) * scale).reshape(n // 8, 8, w)
            for p, c in zip((pick_ref, pick_plain_ref, pick_block_ref), cut)
        ]
        outs[k][...] = jnp.concatenate(parts, axis=1).reshape(3 * n, w)


def add_kernel(a_ref, b_ref, c_ref, d_ref, *outs):
    n = outs[0].shape[0]
    for k, out in enumerate(outs):
        at = slice(k * n, (k + 1) * n)
        out[...] = (a_ref[at, :] + b_ref[at, :]) + (c_ref[at, :] + d_ref[at, :])


def swap(x):
    return lax.all_to_all(x, CTX, 0, 0, tiled=True)


def exchange(blocks, axes=TP):
    return [blocks[0]] + [
        lax.ppermute(blocks[k], axes, [(i, i ^ k) for i in range(4)]) for k in (1, 2, 3)
    ]


def one_hot(rows, columns, match):
    r = lax.broadcasted_iota(jnp.int32, (rows, columns), 0)
    c = lax.broadcasted_iota(jnp.int32, (rows, columns), 1)
    return match(r, c)


def local(
    hidden_in, fac_inner, fac_outer, inv_outer, inv_inner,
    kernel_freq, gate_blocks, mix_first, mix_second, upstream,
):
    rows, width = hidden_in.shape
    inner, outer = fac_inner.shape[0], fac_outer.shape[0]
    ctx = outer // (rows // inner)
    piece = width // 4
    toks = rows // HALVES
    cols = width // ctx
    me = lax.axis_index(TP)
    pair = range(HALVES)

    tall = lambda n: [((piece, n), BF)] * 4

    def plain_of(r):
        return ((r // piece) ^ me) * piece + r % piece

    def block_of(r):
        return (r % piece) * 4 + ((r // piece) ^ me)

    def outer_of(r):
        return (r % (2 * ctx)) // 2 * 4 + r // (2 * ctx) * 2 + r % 2

    def share_of(r):
        near = r // 8
        at = (((near // 16) ^ lax.axis_index("y")) * 4 + ((near // 4 % 4) ^ lax.axis_index("x"))) * 4
        at = at + ((near % 4) ^ lax.axis_index("z_lo"))
        return jnp.where(r % 8 < cols, at * cols + r % 8, -1)

    plain = one_hot(width, width, lambda r, c: plain_of(r) == c).astype(BF)
    block = one_hot(width, width, lambda r, c: block_of(r) == c).astype(BF)
    order = one_hot(outer, outer, lambda r, c: outer_of(r) == c).astype(BF)
    pick = one_hot(ctx * 8, width, lambda r, c: share_of(r) == c).astype(BF)
    pick_plain = one_hot(ctx * 8, width, lambda r, c: share_of(r) == plain_of(c)).astype(BF)
    pick_block = one_hot(ctx * 8, width, lambda r, c: share_of(r) == block_of(c)).astype(BF)

    inner_flops = 2 * toks * width * inner
    fac_inner_t = fac_inner.T
    sent = call(inner_kernel, [((toks, width), BF)], ((hidden_in, 0), fac_inner_t), inner_flops)
    got = [swap(sent[0])]
    up = [
        exchange(call(turn_kernel, tall(toks), ((upstream, i), plain), 2 * toks * width * width, after=sent))
        for i in pair
    ]
    fo, fo_t, io, io_t, first_t, second, second_t = call(
        prepare_kernel, [((outer, outer), BF)] * 4 + [((width, width), BF)] * 3,
        (order, fac_outer, inv_outer, plain, block, mix_first, mix_second),
        8 * outer**3 + 6 * width**3, after=sent,
    )
    freq = kernel_freq.transpose(1, 0, 2)
    inv_inner_t = inv_inner.T
    sent = call(
        inner_kernel, [((toks, width), BF)], ((hidden_in, 1), fac_inner_t), inner_flops,
        after=(up[0][2],),
    )
    got.append(swap(sent[0]))

    half = outer // 2
    eb = 8
    wide = pltpu.VMEM((width // 128, toks, 128), F32)

    def regroup(a, after=()):
        return call(regroup_kernel, [((eb, half, width), BF)], (a,), 0, (wide,), after)[0]

    spec_flops = 2 * 2 * outer * outer * eb * width
    spectrum, *sent = call(
        spectral_kernel,
        [((eb, outer, width), F32), ((toks, width), BF), ((toks, width), BF)],
        (regroup(got[0]), got[1], fo_t, io_t, freq), spec_flops, (wide, wide, wide),
        after=(*up[0], up[1][2], first_t, second, second_t, inv_inner_t, pick, pick_plain, pick_block),
    )
    got = [swap(s) for s in sent]

    conv, gate, mixed, shuf = [], [], [], []
    for i in pair:
        c, g, m, *blocks = call(
            front_kernel,
            [((toks, width), F32), ((toks, width), F32), ((toks, width), BF)] + tall(toks),
            (got[i], inv_inner_t, (hidden_in, i), gate_blocks, first_t),
            2 * toks * width * (inner + 2 * width),
        )
        conv.append(c), gate.append(g), mixed.append(m)
        shuf.append(exchange(blocks))

    outs, bases, got, merged = [], [], [], []
    sums = [0.0, 0.0, 0.0]
    for i in pair:
        shuf_all, gso, *blocks = call(
            middle_kernel,
            [((width, toks), BF)] * 2 + tall(toks) * 2,
            (*shuf[i], *up[i], second, second_t), 2 * toks * width * 2 * width,
        )
        back = exchange(blocks[4:])
        merged.append(exchange(blocks[:4]))
        sent, gm, ggp, gfo = call(
            rear_kernel,
            [((toks, width), BF), ((toks, width), F32), ((toks, width), BF), ((width, toks), BF)],
            (*back, first_t, (upstream, i), gate[i], conv[i], inv_inner),
            2 * toks * width * (inner + width), (pltpu.VMEM((toks, width), BF),),
        )
        got.append(swap(sent))
        turned = dot(jnp.concatenate(merged[i], 0), plain, ((0,), (0,)))
        outs.append((mixed[i].astype(F32) + jax.nn.gelu(turned, approximate=False)).astype(BF))
        bases.append(gm + dot(ggp, gate_blocks, ((1,), (1,))))
        sums[0] += dot(ggp, hidden_in[i * toks : (i + 1) * toks], ((0,), (0,)))
        sums[1] += dot(gfo, mixed[i])
        sums[2] += dot(gso, shuf_all, ((1,), (1,)))

    scale = jnp.full((1,), 1.0 / math.sqrt(rows * ctx), F32)
    shares = ctx * 24
    near = []
    parts = pack(sums, (pick, pick_plain, pick_block, block), scale, shares // 4)
    near.append(exchange(parts, "y"))

    grad_kernel, *sent = call(
        spectral_kernel,
        [((eb, outer, width), F32), ((toks, width), BF), ((toks, width), BF)],
        (regroup(got[0], (merged[0][2],)), got[1], io, fo, freq, spectrum), spec_flops,
        (wide, wide, wide), after=(*merged[0], merged[1][2], near[0][1]),
    )
    got = [swap(s) for s in sent]
    for axis, n in (("x", shares // 16), ("z_lo", shares // 64)):
        parts = call(add_kernel, [((n, width), F32)] * 4, near[-1], 0)
        near.append(exchange(parts, axis))
    grad_input = None
    for i in pair:
        grad_input = finish(got[i], fac_inner, bases[i], i, grad_input, (*merged[1], near[1 + i][1]))
    total, = call(add_kernel, [((24, width), F32)], near[2], 0)
    total = [total[8 * i : 8 * i + cols].T for i in range(3)]
    return (jnp.concatenate(outs, 0), grad_input, grad_kernel.transpose(1, 0, 2), *total)


def pack(sums, tables, scale, rows):
    width = sums[0].shape[1]
    vmem = pl.BlockSpec(memory_space=pltpu.VMEM)
    return pl.pallas_call(
        pack_kernel,
        out_shape=[jax.ShapeDtypeStruct((rows, width), F32)] * 4,
        in_specs=[vmem] * 7 + [pl.BlockSpec(memory_space=pltpu.SMEM)],
        out_specs=[vmem] * 4,
        compiler_params=pltpu.CompilerParams(vmem_limit_bytes=48 * 1024 * 1024),
        cost_estimate=pl.CostEstimate(
            flops=9 * 2 * 4 * rows * width * width, bytes_accessed=24 * rows * width, transcendentals=0
        ),
    )(*sums, *tables, scale)


def finish(got, mat, base, i, whole, after):
    toks, width = got.shape
    vmem = pl.BlockSpec(memory_space=pltpu.VMEM)
    hidden = pl.BlockSpec(memory_space=pl.ANY)
    after = (*after, *([] if whole is None else [whole]))

    def wrapped(got_ref, mat_ref, base_ref, *rest):
        last_kernel(got_ref, mat_ref, base_ref, rest[-1])

    return pl.pallas_call(
        wrapped,
        grid=(1,),
        out_shape=jax.ShapeDtypeStruct((HALVES * toks, width), BF),
        in_specs=[vmem] * 3 + [hidden] * len(after),
        out_specs=pl.BlockSpec((toks, width), lambda g: (i, 0)),
        input_output_aliases={} if whole is None else {2 + len(after): 0},
        compiler_params=pltpu.CompilerParams(vmem_limit_bytes=48 * 1024 * 1024),
        cost_estimate=pl.CostEstimate(
            flops=2 * toks * width * mat.shape[0], bytes_accessed=8 * toks * width, transcendentals=0
        ),
    )(got, mat, base, *after)


def solution(mesh):
    fine = Mesh(mesh.devices.reshape(4, 4, 4, 2, 2), CTX + TP)
    tok = P(CTX, TP)
    mat = P(TP, None)
    small = P(TP, CTX)
    freq = P(None, CTX, TP)
    return jax.shard_map(
        local,
        mesh=fine,
        in_specs=(tok, P(), P(), P(), P(), freq, mat, mat, mat, tok),
        out_specs=(tok, tok, freq, small, small, small),
        check_vma=False,
    )
```

```python
import math

import jax
import jax.numpy as jnp
from jax import lax
from jax.experimental import pallas as pl
from jax.experimental.pallas import tpu as pltpu
from jax.sharding import Mesh
from jax.sharding import PartitionSpec as P

CTX = ("y", "x", "z_lo")
TP = ("z_hi", "core")
HALVES = 2
BF = jnp.bfloat16
F32 = jnp.float32
TILE = 256
VMEM_LIMIT = 24 * 1024 * 1024
ROOT_HALF = math.sqrt(0.5)
INV_ROOT_2PI = 1.0 / math.sqrt(2.0 * math.pi)


def dot(left, right, dims=((1,), (0,)), precision=None):
    return lax.dot_general(
        left, right, (dims, ((), ())), precision=precision, preferred_element_type=F32
    )


def call(body, outs, args, flops, scratch=(), after=()):
    arrays = [a[0] if isinstance(a, tuple) else a for a in args]
    specs = []
    for a in args:
        if isinstance(a, tuple):
            rows, width = a[0].shape
            specs.append(pl.BlockSpec((rows // HALVES, width), lambda g, i=a[1]: (i, 0)))
        else:
            specs.append(pl.BlockSpec(memory_space=pltpu.VMEM))
    halved = any(isinstance(a, tuple) for a in args)
    n, late = len(args), len(after)

    def wrapped(*refs):
        body(*refs[:n], *refs[n + late :])

    moved = sum(a.size * a.dtype.itemsize for a in arrays)
    moved += sum(math.prod(s) * jnp.dtype(d).itemsize for s, d in outs)
    return pl.pallas_call(
        wrapped,
        out_shape=[jax.ShapeDtypeStruct(s, d) for s, d in outs],
        in_specs=specs + [pl.BlockSpec(memory_space=pl.ANY)] * late,
        out_specs=[pl.BlockSpec(memory_space=pltpu.VMEM)] * len(outs),
        scratch_shapes=list(scratch),
        compiler_params=pltpu.CompilerParams(vmem_limit_bytes=VMEM_LIMIT),
        cost_estimate=pl.CostEstimate(
            flops=int(flops), bytes_accessed=int(moved), transcendentals=0
        ),
        **({"grid": (1,)} if halved else {}),
    )(*arrays, *after)


def interleave(parts):
    n, w = parts[0].shape
    cut = [p.reshape(n // 8, 1, 8, w) for p in parts]
    return jnp.concatenate(cut, axis=1).reshape(len(parts) * n, w).astype(BF)


def separate(rows, k):
    n, w = rows.shape
    cut = rows.astype(F32).reshape(n // (8 * k), k, 8, w)
    return [cut[:, i].reshape(n // k, w).astype(BF) for i in range(k)]


def inner_kernel(x_ref, mat_ref, out_ref):
    n = mat_ref.shape[0]
    k = x_ref.shape[0] // n
    for t in range(0, n, TILE):
        part = mat_ref[t : t + TILE, :]
        out_ref[k * t : k * (t + TILE), :] = interleave(
            [dot(part, x_ref[i * n : (i + 1) * n, :]) for i in range(k)]
        )


def widen(got_ref, wide):
    for c in range(wide.shape[0]):
        wide[c] = got_ref[:, c * 128 : (c + 1) * 128].astype(F32)


def rows_of(wide, e):
    parts, n, _ = wide.shape
    return jnp.concatenate(
        [wide[c, pl.ds(e, n // 8, stride=8), :].astype(BF) for c in range(parts)], axis=1
    )


def regroup_kernel(got_ref, out_ref, wide):
    widen(got_ref, wide)
    for e in range(8):
        out_ref[e] = rows_of(wide, e)


def spread(values, e, wide):
    parts, n, _ = wide.shape
    for c in range(parts):
        wide[c, pl.ds(e, n // 8, stride=8), :] = values[:, c * 128 : (c + 1) * 128]


def narrow(wide, out_ref):
    for c in range(wide.shape[0]):
        out_ref[:, c * 128 : (c + 1) * 128] = wide[c].astype(BF)


def there_kernel(got_ref, a_ref, b_ref, freq_ref, spec_ref, out0_ref, out1_ref, wide, back0, back1):
    widen(got_ref, wide)
    m = b_ref.shape[0] // 2
    for e in range(8):
        values = dot(a_ref[...], rows_of(wide, e))
        spec_ref[e] = values
        result = dot(b_ref[...], (values * freq_ref[e].astype(F32)).astype(BF))
        spread(result[:m], e, back0)
        spread(result[m:], e, back1)
    narrow(back0, out0_ref)
    narrow(back1, out1_ref)


def back_kernel(first_ref, got_ref, a_ref, b_ref, freq_ref, spec_ref, grad_ref, out_ref, wide, back):
    widen(got_ref, wide)
    m = a_ref.shape[1] // 2
    for e in range(8):
        values = dot(a_ref[:, :m], first_ref[e]) + dot(a_ref[:, m:], rows_of(wide, e))
        grad_ref[e] = values * spec_ref[e]
        spread(dot(b_ref[...], (values * freq_ref[e].astype(F32)).astype(BF)), e, back)
    narrow(back, out_ref)


def front_kernel(got_ref, mat_ref, x_ref, gate_w_ref, first_t_ref,
                 conv_ref, gate_ref, mixed_ref, s0_ref, s1_ref, s2_ref, s3_ref):
    halves = separate(got_ref[...], 2)
    n = mat_ref.shape[0]
    sends = (s0_ref, s1_ref, s2_ref, s3_ref)
    piece = s0_ref.shape[0]
    for i in range(2):
        for t in range(0, n, TILE):
            at = slice(i * n + t, i * n + t + TILE)
            conv = dot(mat_ref[t : t + TILE, :], halves[i])
            x = x_ref[at, :]
            gate = jax.nn.sigmoid(dot(x, gate_w_ref[...]))
            mixed = (x.astype(F32) + gate * conv).astype(BF)
            conv_ref[at, :] = conv
            gate_ref[at, :] = gate
            mixed_ref[at, :] = mixed
            first = dot(first_t_ref[...], mixed, ((1,), (1,))).astype(BF)
            for k in range(4):
                sends[k][:, at] = first[k * piece : (k + 1) * piece, :]


def middle_kernel(*refs):
    shuf, up = refs[:4], refs[4:8]
    w_ref, wt_ref = refs[8:10]
    all_ref, gso_ref = refs[10:12]
    merged, back = refs[12:16], refs[16:20]
    piece, n = shuf[0].shape
    for t in range(0, n, TILE):
        at = slice(t, t + TILE)
        xs = jnp.concatenate([r[:, at] for r in shuf], axis=0)
        ups = jnp.concatenate([r[:, at] for r in up], axis=0)
        all_ref[:, at] = xs
        out = dot(wt_ref[...], xs).astype(BF)
        m = out.astype(F32)
        slope = 0.5 * (1.0 + lax.erf(m * ROOT_HALF)) + m * (INV_ROOT_2PI * jnp.exp(-0.5 * m * m))
        gso = (ups.astype(F32) * slope).astype(BF)
        gso_ref[:, at] = gso
        gsh = dot(w_ref[...], gso).astype(BF)
        for k in range(4):
            merged[k][:, at] = out[k * piece : (k + 1) * piece, :]
            back[k][:, at] = gsh[k * piece : (k + 1) * piece, :]


def rear_kernel(g0_ref, g1_ref, g2_ref, g3_ref, first_t_ref, up_ref, gate_ref, conv_ref, mat_ref,
                out_ref, gm_ref, ggp_ref, gfo_ref, scratch):
    n = mat_ref.shape[0]
    for t in range(0, 2 * n, TILE):
        at = slice(t, t + TILE)
        gfo = jnp.concatenate([r[:, at] for r in (g0_ref, g1_ref, g2_ref, g3_ref)], axis=0)
        gfo_ref[:, at] = gfo
        gm = up_ref[at, :].astype(F32) + dot(gfo, first_t_ref[...], ((0,), (0,)))
        gate = gate_ref[at, :]
        opened = gm * gate
        scratch[at, :] = opened.astype(BF)
        gm_ref[at, :] = gm
        ggp_ref[at, :] = (opened * conv_ref[at, :] * (1.0 - gate)).astype(BF)
    for t in range(0, n, TILE):
        part = mat_ref[t : t + TILE, :]
        out_ref[2 * t : 2 * (t + TILE), :] = interleave(
            [dot(part, scratch[i * n : (i + 1) * n, :]) for i in range(2)]
        )


def last_kernel(got_ref, mat_ref, base0_ref, base1_ref, out_ref):
    n = mat_ref.shape[0]
    bases = (base0_ref, base1_ref)
    for i, part in enumerate(separate(got_ref[...], 4)):
        for t in range(0, n, TILE):
            at = slice(i % 2 * n + t, i % 2 * n + t + TILE)
            value = bases[i // 2][at, :] + dot(mat_ref[t : t + TILE, :], part)
            out_ref[i * n + t : i * n + t + TILE, :] = value.astype(BF)


def turn_kernel(x_ref, plain_ref, *sends):
    piece, n = sends[0].shape
    for t in range(0, n, TILE):
        at = slice(t, t + TILE)
        turned = dot(plain_ref[...], x_ref[at, :], ((1,), (1,))).astype(BF)
        for k in range(4):
            sends[k][:, at] = turned[k * piece : (k + 1) * piece, :]


def prepare_kernel(order_ref, io_ref, plain_ref, block_ref, mix1_ref, mix2_ref,
                   io_out, io_t_out, first_t_out, second_out, second_t_out):
    order = order_ref[...]
    io = dot(io_ref[...], order, ((1,), (1,)))
    io_out[...] = io.astype(BF)
    io_t_out[...] = io.T.astype(BF)
    first_t_out[...] = dot(plain_ref[...], mix1_ref[...], ((1,), (1,))).astype(BF)
    block = block_ref[...]
    second = dot(dot(block, mix2_ref[...]).astype(BF), block, ((1,), (1,)))
    second_out[...] = second.astype(BF)
    second_t_out[...] = second.T.astype(BF)


def thirds(x):
    high = x.astype(BF)
    rest = x - high.astype(F32)
    middle = rest.astype(BF)
    return high, middle, (rest - middle.astype(F32)).astype(BF)


def pack_kernel(s0_ref, s1_ref, s2_ref, pick_ref, pick_plain_ref, pick_block_ref, block_ref, scale_ref,
                *outs):
    scale = scale_ref[0]
    s2 = sum(dot(p, block_ref[...]) for p in thirds(s2_ref[...]))
    cut = [thirds(s0_ref[...]), thirds(s1_ref[...]), thirds(s2)]
    w = s0_ref.shape[1]
    n = pick_ref.shape[0] // 4
    for k in range(4):
        parts = [
            (sum(dot(p[k * n : (k + 1) * n, :], x) for x in c) * scale).reshape(n // 8, 8, w)
            for p, c in zip((pick_ref, pick_plain_ref, pick_block_ref), cut)
        ]
        outs[k][...] = jnp.concatenate(parts, axis=1).reshape(3 * n, w)


def add_kernel(a_ref, b_ref, c_ref, d_ref, *outs):
    n = outs[0].shape[0]
    for k, out in enumerate(outs):
        at = slice(k * n, (k + 1) * n)
        out[...] = (a_ref[at, :] + b_ref[at, :]) + (c_ref[at, :] + d_ref[at, :])


def swap(x):
    return lax.all_to_all(x, CTX, 0, 0, tiled=True)


def exchange(blocks, axes=TP):
    return [blocks[0]] + [
        lax.ppermute(blocks[k], axes, [(i, i ^ k) for i in range(4)]) for k in (1, 2, 3)
    ]


def one_hot(rows, columns, match):
    r = lax.broadcasted_iota(jnp.int32, (rows, columns), 0)
    c = lax.broadcasted_iota(jnp.int32, (rows, columns), 1)
    return match(r, c)


def local(
    hidden_in, fac_inner, fac_outer, inv_outer, inv_inner,
    kernel_freq, gate_blocks, mix_first, mix_second, upstream,
):
    rows, width = hidden_in.shape
    inner, outer = fac_inner.shape[0], fac_outer.shape[0]
    ctx = outer // (rows // inner)
    piece = width // 4
    toks = rows // HALVES
    cols = width // ctx
    me = lax.axis_index(TP)
    pair = range(HALVES)

    tall = lambda n: [((piece, n), BF)] * 4

    def plain_of(r):
        return ((r // piece) ^ me) * piece + r % piece

    def block_of(r):
        return (r % piece) * 4 + ((r // piece) ^ me)

    def outer_of(r):
        return (r % (2 * ctx)) // 2 * 4 + r // (2 * ctx) * 2 + r % 2

    def share_of(r):
        near = r // 8
        at = (((near // 16) ^ lax.axis_index("y")) * 4 + ((near // 4 % 4) ^ lax.axis_index("x"))) * 4
        at = at + ((near % 4) ^ lax.axis_index("z_lo"))
        return jnp.where(r % 8 < cols, at * cols + r % 8, -1)

    plain = one_hot(width, width, lambda r, c: plain_of(r) == c).astype(BF)
    block = one_hot(width, width, lambda r, c: block_of(r) == c).astype(BF)
    order = one_hot(outer, outer, lambda r, c: outer_of(r) == c).astype(BF)
    pick = one_hot(ctx * 8, width, lambda r, c: share_of(r) == c).astype(BF)
    pick_plain = one_hot(ctx * 8, width, lambda r, c: share_of(r) == plain_of(c)).astype(BF)
    pick_block = one_hot(ctx * 8, width, lambda r, c: share_of(r) == block_of(c)).astype(BF)

    inner_flops = 2 * rows * width * inner
    sent = call(inner_kernel, [((rows, width), BF)], (hidden_in, fac_inner.T), inner_flops)
    got = swap(sent[0])
    up = [
        exchange(call(turn_kernel, tall(toks), ((upstream, i), plain), 2 * toks * width * width, after=sent))
        for i in pair
    ]
    io, io_t, first_t, second, second_t = call(
        prepare_kernel, [((outer, outer), BF)] * 2 + [((width, width), BF)] * 3,
        (order, inv_outer, plain, block, mix_first, mix_second),
        4 * outer**3 + 6 * width**3, after=sent,
    )
    freq = kernel_freq.transpose(1, 0, 2)
    inv_inner_t = inv_inner.T

    half = outer // 2
    eb = 8
    wide = pltpu.VMEM((width // 128, rows, 128), F32)
    thin = pltpu.VMEM((width // 128, toks, 128), F32)
    spec_flops = 2 * 2 * outer * outer * eb * width
    spectrum, *sent = call(
        there_kernel,
        [((eb, outer, width), F32), ((toks, width), BF), ((toks, width), BF)],
        (got, fac_outer.T, io_t, freq), spec_flops, (wide, thin, thin),
        after=(*up[0], up[1][2], first_t, second, second_t, inv_inner_t, pick, pick_plain, pick_block),
    )
    got = [swap(s) for s in sent]

    conv, gate, mixed, shuf = [], [], [], []
    for i in pair:
        c, g, m, *blocks = call(
            front_kernel,
            [((toks, width), F32), ((toks, width), F32), ((toks, width), BF)] + tall(toks),
            (got[i], inv_inner_t, (hidden_in, i), gate_blocks, first_t),
            2 * toks * width * (inner + 2 * width),
        )
        conv.append(c), gate.append(g), mixed.append(m)
        shuf.append(exchange(blocks))

    outs, bases, got, merged, middle, back = [], [], [], [], [], []
    sums = [0.0, 0.0, 0.0]
    for i in pair:
        middle.append(call(
            middle_kernel,
            [((width, toks), BF)] * 2 + tall(toks) * 2,
            (*shuf[i], *up[i], second, second_t), 2 * toks * width * 2 * width,
            after=(shuf[1][1],),
        ))
        back.append(exchange(middle[i][6:]))
    for i in pair:
        shuf_all, gso, *blocks = middle[i]
        sent, gm, ggp, gfo = call(
            rear_kernel,
            [((toks, width), BF), ((toks, width), F32), ((toks, width), BF), ((width, toks), BF)],
            (*back[i], first_t, (upstream, i), gate[i], conv[i], inv_inner),
            2 * toks * width * (inner + width), (pltpu.VMEM((toks, width), BF),),
            after=(middle[1][1],),
        )
        merged.append(exchange(blocks[:4]))
        got.append(swap(sent))
        turned = dot(jnp.concatenate(merged[i], 0), plain, ((0,), (0,)))
        outs.append((mixed[i].astype(F32) + jax.nn.gelu(turned, approximate=False)).astype(BF))
        bases.append(gm + dot(ggp, gate_blocks, ((1,), (1,))))
        sums[0] += dot(ggp, hidden_in[i * toks : (i + 1) * toks], ((0,), (0,)))
        sums[1] += dot(gfo, mixed[i])
        sums[2] += dot(gso, shuf_all, ((1,), (1,)))

    scale = jnp.full((1,), 1.0 / math.sqrt(rows * ctx), F32)
    shares = ctx * 24
    near = []
    parts = pack(sums, (pick, pick_plain, pick_block, block), scale, shares // 4)
    near.append(exchange(parts, "y"))

    first = call(regroup_kernel, [((eb, half, width), BF)], (got[0],), 0, (thin,), (merged[0][2],))[0]
    grad_kernel, sent = call(
        back_kernel, [((eb, outer, width), F32), ((rows, width), BF)],
        (first, got[1], io, fac_outer, freq, spectrum), spec_flops, (thin, wide),
        after=(*merged[0], merged[1][2], *near[0]),
    )
    got = swap(sent)
    grad_kernel = grad_kernel.transpose(1, 0, 2)
    for axis, n in (("x", shares // 16), ("z_lo", shares // 64)):
        parts = call(add_kernel, [((n, width), F32)] * 4, near[-1], 0)
        near.append(exchange(parts, axis))
    total, = call(add_kernel, [((24, width), F32)], near[2], 0)
    total = [total[8 * i : 8 * i + cols].T for i in range(3)]
    layer_out = jnp.concatenate(outs, 0)
    grad_input, = call(
        last_kernel, [((rows, width), BF)], (got, fac_inner, *bases), inner_flops,
        after=(grad_kernel, layer_out, *total),
    )
    return (layer_out, grad_input, grad_kernel, *total)


def pack(sums, tables, scale, rows):
    width = sums[0].shape[1]
    vmem = pl.BlockSpec(memory_space=pltpu.VMEM)
    return pl.pallas_call(
        pack_kernel,
        out_shape=[jax.ShapeDtypeStruct((rows, width), F32)] * 4,
        in_specs=[vmem] * 7 + [pl.BlockSpec(memory_space=pltpu.SMEM)],
        out_specs=[vmem] * 4,
        compiler_params=pltpu.CompilerParams(vmem_limit_bytes=VMEM_LIMIT),
        cost_estimate=pl.CostEstimate(
            flops=9 * 2 * 4 * rows * width * width, bytes_accessed=24 * rows * width, transcendentals=0
        ),
    )(*sums, *tables, scale)


def solution(mesh):
    fine = Mesh(mesh.devices.reshape(4, 4, 4, 2, 2), CTX + TP)
    tok = P(CTX, TP)
    mat = P(TP, None)
    small = P(TP, CTX)
    freq = P(None, CTX, TP)
    return jax.shard_map(
        local,
        mesh=fine,
        in_specs=(tok, P(), P(), P(), P(), freq, mat, mat, mat, tok),
        out_specs=(tok, tok, freq, small, small, small),
        check_vma=False,
    )
```

```python
import functools
import math

import jax
import jax.numpy as jnp
from jax import lax
from jax.experimental import pallas as pl
from jax.experimental.pallas import tpu as pltpu
from jax.sharding import Mesh
from jax.sharding import PartitionSpec as P

CTX = ("y", "x", "z_lo")
TP = ("z_hi", "core")
HALVES = 2
BF = jnp.bfloat16
F32 = jnp.float32
TILE = 256
VMEM_LIMIT = 64 * 1024 * 1024
ROOT_HALF = math.sqrt(0.5)
INV_ROOT_2PI = 1.0 / math.sqrt(2.0 * math.pi)


def dot(left, right, dims=((1,), (0,)), precision=None):
    return lax.dot_general(
        left, right, (dims, ((), ())), precision=precision, preferred_element_type=F32
    )


def whole(array):
    return array, array.shape, lambda g: (0,) * len(array.shape)


def rows_at(array, n, start=0):
    return array, (n,) + array.shape[1:], lambda g: (start + g,) + (0,) * (len(array.shape) - 1)


def columns_at(array, n):
    return array, (array.shape[0], n), lambda g: (0, g)


def call(body, steps, args, outs, flops, scratch=(), after=()):
    arrays = [a[0] for a in args]
    n, late = len(args), len(after)

    def wrapped(*refs):
        body(*refs[:n], *refs[n + late :])

    moved = sum(math.prod(a.shape) * jnp.dtype(a.dtype).itemsize for a in arrays + [o[0] for o in outs])
    return pl.pallas_call(
        wrapped,
        grid=(steps,),
        out_shape=[o[0] for o in outs],
        in_specs=[pl.BlockSpec(a[1], a[2]) for a in args] + [pl.BlockSpec(memory_space=pl.ANY)] * late,
        out_specs=[pl.BlockSpec(o[1], o[2]) for o in outs],
        scratch_shapes=list(scratch),
        compiler_params=pltpu.CompilerParams(vmem_limit_bytes=VMEM_LIMIT),
        cost_estimate=pl.CostEstimate(
            flops=int(flops), bytes_accessed=int(moved), transcendentals=0
        ),
    )(*arrays, *after)


def interleave(parts):
    n, w = parts[0].shape
    cut = [p.reshape(n // 8, 1, 8, w) for p in parts]
    return jnp.concatenate(cut, axis=1).reshape(len(parts) * n, w).astype(BF)


def separate(rows, k):
    n, w = rows.shape
    cut = rows.astype(F32).reshape(n // (8 * k), k, 8, w)
    return [cut[:, i].reshape(n // k, w).astype(BF) for i in range(k)]


def inner_kernel(x_ref, mat_ref, out_ref):
    n = mat_ref.shape[0]
    part = mat_ref[...]
    blocks = [x_ref[i * n : (i + 1) * n, :] for i in range(x_ref.shape[0] // n)]
    out_ref[...] = interleave([dot(part, x, ((0,), (0,))) for x in blocks])


def widen(got_ref, wide):
    for c in range(wide.shape[0]):
        wide[c] = got_ref[:, c * 128 : (c + 1) * 128].astype(F32)


def rows_of(wide, e):
    parts, n, _ = wide.shape
    return jnp.concatenate(
        [wide[c, pl.ds(e, n // 8, stride=8), :].astype(BF) for c in range(parts)], axis=1
    )


def regroup_kernel(got_ref, out_ref, wide):
    widen(got_ref, wide)
    for e in range(8):
        out_ref[e] = rows_of(wide, e)


def spread(values, e, wide):
    parts, n, _ = wide.shape
    for c in range(parts):
        wide[c, pl.ds(e, n // 8, stride=8), :] = values[:, c * 128 : (c + 1) * 128]


def narrow(wide, out_ref):
    for c in range(wide.shape[0]):
        out_ref[:, c * 128 : (c + 1) * 128] = wide[c].astype(BF)


def there_kernel(got_ref, a_ref, b_ref, freq_ref, spec_ref, out0_ref, out1_ref, wide, back0, back1):
    e = pl.program_id(0)

    @pl.when(e == 0)
    def _():
        widen(got_ref, wide)

    m = b_ref.shape[0] // 2
    values = dot(a_ref[...], rows_of(wide, e))
    spec_ref[0] = values
    result = dot(b_ref[...], (values * freq_ref[0].astype(F32)).astype(BF))
    spread(result[:m], e, back0)
    spread(result[m:], e, back1)

    @pl.when(e == 7)
    def _():
        narrow(back0, out0_ref)
        narrow(back1, out1_ref)


def back_kernel(first_ref, got_ref, a_ref, b_ref, freq_ref, spec_ref, grad_ref, out_ref, wide, back):
    e = pl.program_id(0)

    @pl.when(e == 0)
    def _():
        widen(got_ref, wide)

    m = a_ref.shape[1] // 2
    values = dot(a_ref[:, :m], first_ref[0]) + dot(a_ref[:, m:], rows_of(wide, e))
    grad_ref[0] = values * spec_ref[0]
    spread(dot(b_ref[...], (values * freq_ref[0].astype(F32)).astype(BF)), e, back)

    @pl.when(e == 7)
    def _():
        narrow(back, out_ref)


def front_kernel(got_ref, mat_ref, x_ref, gate_w_ref, first_t_ref,
                 conv_ref, gate_ref, mixed_ref, s0_ref, s1_ref, s2_ref, s3_ref, parts):
    t = pl.program_id(0)
    n = mat_ref.shape[1]
    piece = s0_ref.shape[0]

    @pl.when(t == 0)
    def _():
        for i, part in enumerate(separate(got_ref[...], 2)):
            parts[i * n : (i + 1) * n, :] = part

    conv = dot(mat_ref[...], parts[pl.ds(pl.multiple_of(t // 2 * n, n), n), :])
    x = x_ref[...]
    gate = jax.nn.sigmoid(dot(x, gate_w_ref[...]))
    mixed = (x.astype(F32) + gate * conv).astype(BF)
    conv_ref[...] = conv
    gate_ref[...] = gate
    mixed_ref[...] = mixed
    first = dot(first_t_ref[...], mixed, ((1,), (1,))).astype(BF)
    for k, send in enumerate((s0_ref, s1_ref, s2_ref, s3_ref)):
        send[...] = first[k * piece : (k + 1) * piece, :]


def middle_kernel(*refs):
    shuf, up = refs[:4], refs[4:8]
    w_ref, wt_ref = refs[8:10]
    all_ref, gso_ref = refs[10:12]
    merged, back = refs[12:16], refs[16:20]
    piece = shuf[0].shape[0]
    xs = jnp.concatenate([r[...] for r in shuf], axis=0)
    ups = jnp.concatenate([r[...] for r in up], axis=0)
    all_ref[...] = xs
    out = dot(wt_ref[...], xs).astype(BF)
    m = out.astype(F32)
    slope = 0.5 * (1.0 + lax.erf(m * ROOT_HALF)) + m * (INV_ROOT_2PI * jnp.exp(-0.5 * m * m))
    gso = (ups.astype(F32) * slope).astype(BF)
    gso_ref[...] = gso
    gsh = dot(w_ref[...], gso).astype(BF)
    for k in range(4):
        merged[k][...] = out[k * piece : (k + 1) * piece, :]
        back[k][...] = gsh[k * piece : (k + 1) * piece, :]


def rear_kernel(g0_ref, g1_ref, g2_ref, g3_ref, first_t_ref, up_ref, gate_ref, conv_ref, mat_ref,
                out_ref, gm_ref, ggp_ref, gfo_ref, opened_all):
    step = pl.program_id(0)
    n = mat_ref.shape[0]
    rows = up_ref.shape[0]
    gfo = jnp.concatenate([r[...] for r in (g0_ref, g1_ref, g2_ref, g3_ref)], axis=0)
    gfo_ref[...] = gfo
    gm = up_ref[...].astype(F32) + dot(gfo, first_t_ref[...], ((0,), (0,)))
    gate = gate_ref[...]
    opened = gm * gate
    opened_all[pl.ds(pl.multiple_of(step * rows, rows), rows), :] = opened.astype(BF)
    gm_ref[...] = gm
    ggp_ref[...] = (opened * conv_ref[...] * (1.0 - gate)).astype(BF)

    @pl.when(step == 2 * n // rows - 1)
    def _():
        for t in range(0, n, TILE):
            part = mat_ref[t : t + TILE, :]
            out_ref[2 * t : 2 * (t + TILE), :] = interleave(
                [dot(part, opened_all[i * n : (i + 1) * n, :]) for i in range(2)]
            )


def last_kernel(got_ref, mat_ref, base0_ref, base1_ref, out_ref, parts):
    a = pl.program_id(0)
    n = mat_ref.shape[0]

    @pl.when(a == 0)
    def _():
        for i, part in enumerate(separate(got_ref[...], 4)):
            parts[i * n : (i + 1) * n, :] = part

    conv_back = dot(mat_ref[...], parts[pl.ds(pl.multiple_of(a * n, n), n), :])

    @pl.when(a < 2)
    def _():
        out_ref[...] = (base0_ref[...] + conv_back).astype(BF)

    @pl.when(a >= 2)
    def _():
        out_ref[...] = (base1_ref[...] + conv_back).astype(BF)


def turn_kernel(x_ref, plain_ref, *sends):
    piece = sends[0].shape[0]
    turned = dot(plain_ref[...], x_ref[...], ((1,), (1,))).astype(BF)
    for k in range(4):
        sends[k][...] = turned[k * piece : (k + 1) * piece, :]


def prepare_kernel(order_ref, io_ref, plain_ref, block_ref, mix1_ref, mix2_ref,
                   io_out, io_t_out, first_t_out, second_out, second_t_out):
    order = order_ref[...]
    io = dot(io_ref[...], order, ((1,), (1,)))
    io_out[...] = io.astype(BF)
    io_t_out[...] = io.T.astype(BF)
    first_t_out[...] = dot(plain_ref[...], mix1_ref[...], ((1,), (1,))).astype(BF)
    block = block_ref[...]
    second = dot(dot(block, mix2_ref[...]).astype(BF), block, ((1,), (1,)))
    second_out[...] = second.astype(BF)
    second_t_out[...] = second.T.astype(BF)


def thirds(x):
    high = x.astype(BF)
    rest = x - high.astype(F32)
    middle = rest.astype(BF)
    return high, middle, (rest - middle.astype(F32)).astype(BF)


def pack_kernel(s0_ref, s1_ref, s2_ref, pick_ref, pick_plain_ref, pick_block_ref, block_ref,
                *outs, scale):
    s2 = sum(dot(p, block_ref[...]) for p in thirds(s2_ref[...]))
    cut = [thirds(s0_ref[...]), thirds(s1_ref[...]), thirds(s2)]
    w = s0_ref.shape[1]
    n = pick_ref.shape[0] // 4
    for k in range(4):
        parts = [
            (sum(dot(p[k * n : (k + 1) * n, :], x) for x in c) * scale).reshape(n // 8, 8, w)
            for p, c in zip((pick_ref, pick_plain_ref, pick_block_ref), cut)
        ]
        outs[k][...] = jnp.concatenate(parts, axis=1).reshape(3 * n, w)


def add_kernel(a_ref, b_ref, c_ref, d_ref, *outs):
    n = outs[0].shape[0]
    for k, out in enumerate(outs):
        at = slice(k * n, (k + 1) * n)
        out[...] = (a_ref[at, :] + b_ref[at, :]) + (c_ref[at, :] + d_ref[at, :])


def swap(x):
    return lax.all_to_all(x, CTX, 0, 0, tiled=True)


def exchange(blocks, axes=TP):
    return [blocks[0]] + [
        lax.ppermute(blocks[k], axes, [(i, i ^ k) for i in range(4)]) for k in (1, 2, 3)
    ]


def one_hot(rows, columns, match):
    r = lax.broadcasted_iota(jnp.int32, (rows, columns), 0)
    c = lax.broadcasted_iota(jnp.int32, (rows, columns), 1)
    return match(r, c)


def local(
    hidden_in, fac_inner, fac_outer, inv_outer, inv_inner,
    kernel_freq, gate_blocks, mix_first, mix_second, upstream,
):
    rows, width = hidden_in.shape
    inner, outer = fac_inner.shape[0], fac_outer.shape[0]
    ctx = outer // (rows // inner)
    piece = width // 4
    toks = rows // HALVES
    cols = width // ctx
    me = lax.axis_index(TP)
    pair = range(HALVES)

    def shape(*dims, dtype=BF):
        return jax.ShapeDtypeStruct(dims, dtype)

    tall = [columns_at(shape(piece, toks), TILE)] * 4
    sheet = shape(toks, width)
    wide_sheet = shape(toks, width, dtype=F32)
    tiles = toks // TILE

    def plain_of(r):
        return ((r // piece) ^ me) * piece + r % piece

    def block_of(r):
        return (r % piece) * 4 + ((r // piece) ^ me)

    def outer_of(r):
        return (r % (2 * ctx)) // 2 * 4 + r // (2 * ctx) * 2 + r % 2

    def share_of(r):
        near = r // 8
        at = (((near // 16) ^ lax.axis_index("y")) * 4 + ((near // 4 % 4) ^ lax.axis_index("x"))) * 4
        at = at + ((near % 4) ^ lax.axis_index("z_lo"))
        return jnp.where(r % 8 < cols, at * cols + r % 8, -1)

    plain = one_hot(width, width, lambda r, c: plain_of(r) == c).astype(BF)
    block = one_hot(width, width, lambda r, c: block_of(r) == c).astype(BF)
    order = one_hot(outer, outer, lambda r, c: outer_of(r) == c).astype(BF)
    pick = one_hot(ctx * 8, width, lambda r, c: share_of(r) == c).astype(BF)
    pick_plain = one_hot(ctx * 8, width, lambda r, c: share_of(r) == plain_of(c)).astype(BF)
    pick_block = one_hot(ctx * 8, width, lambda r, c: share_of(r) == block_of(c)).astype(BF)

    inner_flops = 2 * rows * width * inner
    sent = call(
        inner_kernel, 4, [whole(hidden_in), columns_at(fac_inner, inner // 4)],
        [rows_at(shape(rows, width), rows // 4)], inner_flops,
    )
    got = swap(sent[0])
    up = [
        exchange(call(
            turn_kernel, tiles, [rows_at(upstream, TILE, i * tiles), whole(plain)], tall,
            2 * toks * width * width, after=sent,
        ))
        for i in pair
    ]
    square = whole(shape(width, width))
    io, io_t, first_t, second, second_t = call(
        prepare_kernel, 1, [whole(m) for m in (order, inv_outer, plain, block, mix_first, mix_second)],
        [whole(shape(outer, outer))] * 2 + [square] * 3, 4 * outer**3 + 6 * width**3, after=sent,
    )
    freq = kernel_freq.transpose(1, 0, 2)
    inv_inner_t = inv_inner.T

    half = outer // 2
    eb = 8
    wide = pltpu.VMEM((width // 128, rows, 128), F32)
    thin = pltpu.VMEM((width // 128, toks, 128), F32)
    spec_flops = 2 * 2 * outer * outer * eb * width
    spectrum, *sent = call(
        there_kernel, eb, [whole(got), whole(fac_outer.T), whole(io_t), rows_at(freq, 1)],
        [rows_at(shape(eb, outer, width, dtype=F32), 1), whole(sheet), whole(sheet)],
        spec_flops, (wide, thin, thin),
        after=(*up[0][2:], *up[1][2:], first_t, second, second_t, inv_inner_t, pick, pick_plain, pick_block),
    )
    got = [swap(s) for s in sent]

    conv, gate, mixed, shuf = [], [], [], []
    for i in pair:
        c, g, m, *blocks = call(
            front_kernel, tiles,
            [whole(got[i]), (inv_inner_t, (TILE, inner), lambda t: (t % 2, 0)),
             rows_at(hidden_in, TILE, i * tiles), whole(gate_blocks), whole(first_t)],
            [rows_at(wide_sheet, TILE), rows_at(wide_sheet, TILE), rows_at(sheet, TILE)] + tall,
            2 * toks * width * (inner + 2 * width), (pltpu.VMEM((toks, width), BF),),
            after=tuple(shuf[0][2:3]) if shuf else (),
        )
        conv.append(c), gate.append(g), mixed.append(m)
        shuf.append(exchange(blocks))

    outs, bases, got, merged, middle, back = [], [], [], [], [], []
    sums = [0.0, 0.0, 0.0]
    for i in pair:
        middle.append(call(
            middle_kernel, tiles,
            [columns_at(b, TILE) for b in (*shuf[i], *up[i])] + [whole(second), whole(second_t)],
            [columns_at(shape(width, toks), TILE)] * 2 + tall * 2, 2 * toks * width * 2 * width,
            after=(mixed[1], shuf[1][1]),
        ))
        back.append(exchange(middle[i][6:]))
    for i in pair:
        shuf_all, gso, *blocks = middle[i]
        sent, gm, ggp, gfo = call(
            rear_kernel, tiles,
            [columns_at(b, TILE) for b in back[i]]
            + [whole(first_t), rows_at(upstream, TILE, i * tiles), rows_at(gate[i], TILE),
               rows_at(conv[i], TILE), whole(inv_inner)],
            [whole(sheet), rows_at(wide_sheet, TILE), rows_at(sheet, TILE),
             columns_at(shape(width, toks), TILE)],
            2 * toks * width * (inner + width), (pltpu.VMEM((toks, width), BF),),
            after=(middle[1][1],),
        )
        merged.append(exchange(blocks[:4]))
        got.append(swap(sent))
        turned = dot(jnp.concatenate(merged[i], 0), plain, ((0,), (0,)))
        outs.append((mixed[i].astype(F32) + jax.nn.gelu(turned, approximate=False)).astype(BF))
        bases.append(gm + dot(ggp, gate_blocks, ((1,), (1,))))
        sums[0] += dot(ggp, hidden_in[i * toks : (i + 1) * toks], ((0,), (0,)))
        sums[1] += dot(gfo, mixed[i])
        sums[2] += dot(gso, shuf_all, ((1,), (1,)))

    shares = ctx * 24
    near = []

    def share(n):
        return whole(shape(n, width, dtype=F32))

    parts = call(
        functools.partial(pack_kernel, scale=1.0 / math.sqrt(rows * ctx)), 1,
        [whole(m) for m in (*sums, pick, pick_plain, pick_block, block)], [share(shares // 4)] * 4,
        18 * shares * width * width,
    )
    near.append(exchange(parts, "y"))

    first, = call(
        regroup_kernel, 1, [whole(got[0])], [whole(shape(eb, half, width))], 0, (thin,),
    )
    grad_kernel, sent = call(
        back_kernel, eb,
        [rows_at(first, 1), whole(got[1]), whole(io), whole(fac_outer), rows_at(freq, 1), rows_at(spectrum, 1)],
        [rows_at(shape(eb, outer, width, dtype=F32), 1), whole(shape(rows, width))],
        spec_flops, (thin, wide), after=tuple(near[0][1:]),
    )
    got = swap(sent)
    grad_kernel = grad_kernel.transpose(1, 0, 2)
    for axis, n in (("x", shares // 16), ("z_lo", shares // 64)):
        parts = call(add_kernel, 1, [whole(p) for p in near[-1]], [share(n)] * 4, 0)
        near.append(exchange(parts, axis))
    total, = call(add_kernel, 1, [whole(p) for p in near[2]], [share(24)], 0)
    total = [total[8 * i : 8 * i + cols].T for i in range(3)]
    layer_out = jnp.concatenate(outs, 0)
    grad_input, = call(
        last_kernel, 4,
        [whole(got), whole(fac_inner), (bases[0], (inner, width), lambda a: (jnp.minimum(a, 1), 0)),
         (bases[1], (inner, width), lambda a: (jnp.maximum(a - 2, 0), 0))],
        [rows_at(shape(rows, width), inner)], inner_flops, (pltpu.VMEM((rows, width), BF),),
        after=(grad_kernel, layer_out, *total),
    )
    return (layer_out, grad_input, grad_kernel, *total)


def solution(mesh):
    fine = Mesh(mesh.devices.reshape(4, 4, 4, 2, 2), CTX + TP)
    tok = P(CTX, TP)
    mat = P(TP, None)
    small = P(TP, CTX)
    freq = P(None, CTX, TP)
    return jax.shard_map(
        local,
        mesh=fine,
        in_specs=(tok, P(), P(), P(), P(), freq, mat, mat, mat, tok),
        out_specs=(tok, tok, freq, small, small, small),
        check_vma=False,
    )
```

```python
import functools
import math

import jax
import jax.numpy as jnp
from jax import lax
from jax.experimental import pallas as pl
from jax.experimental.pallas import tpu as pltpu
from jax.sharding import Mesh
from jax.sharding import PartitionSpec as P

CTX = ("y", "x", "z_lo")
TP = ("z_hi", "core")
HALVES = 2
BF = jnp.bfloat16
F32 = jnp.float32
TILE = 512
VMEM_LIMIT = 64 * 1024 * 1024
ROOT_HALF = math.sqrt(0.5)
INV_ROOT_2PI = 1.0 / math.sqrt(2.0 * math.pi)


def dot(left, right, dims=((1,), (0,)), precision=None):
    return lax.dot_general(
        left, right, (dims, ((), ())), precision=precision, preferred_element_type=F32
    )


def whole(array):
    return array, array.shape, lambda g: (0,) * len(array.shape)


def rows_at(array, n, start=0):
    return array, (n,) + array.shape[1:], lambda g: (start + g,) + (0,) * (len(array.shape) - 1)


def columns_at(array, n):
    return array, (array.shape[0], n), lambda g: (0, g)


def call(body, steps, args, outs, flops, scratch=(), after=()):
    arrays = [a[0] for a in args]
    n, late = len(args), len(after)

    def wrapped(*refs):
        body(*refs[:n], *refs[n + late :])

    moved = sum(math.prod(a.shape) * jnp.dtype(a.dtype).itemsize for a in arrays + [o[0] for o in outs])
    return pl.pallas_call(
        wrapped,
        grid=(steps,),
        out_shape=[o[0] for o in outs],
        in_specs=[pl.BlockSpec(a[1], a[2]) for a in args] + [pl.BlockSpec(memory_space=pl.ANY)] * late,
        out_specs=[pl.BlockSpec(o[1], o[2]) for o in outs],
        scratch_shapes=list(scratch),
        compiler_params=pltpu.CompilerParams(vmem_limit_bytes=VMEM_LIMIT),
        cost_estimate=pl.CostEstimate(
            flops=int(flops), bytes_accessed=int(moved), transcendentals=0
        ),
    )(*arrays, *after)


def interleave(parts):
    n, w = parts[0].shape
    cut = [p.reshape(n // 8, 1, 8, w) for p in parts]
    return jnp.concatenate(cut, axis=1).reshape(len(parts) * n, w).astype(BF)


def separate(rows, k):
    n, w = rows.shape
    cut = rows.astype(F32).reshape(n // (8 * k), k, 8, w)
    return [cut[:, i].reshape(n // k, w).astype(BF) for i in range(k)]


def inner_kernel(x_ref, mat_ref, out_ref):
    n = mat_ref.shape[0]
    part = mat_ref[...]
    blocks = [x_ref[i * n : (i + 1) * n, :] for i in range(x_ref.shape[0] // n)]
    out_ref[...] = interleave([dot(part, x, ((0,), (0,))) for x in blocks])


def widen(got_ref, wide):
    for c in range(wide.shape[0]):
        wide[c] = got_ref[:, c * 128 : (c + 1) * 128].astype(F32)


def rows_of(wide, e):
    parts, n, _ = wide.shape
    return jnp.concatenate(
        [wide[c, pl.ds(e, n // 8, stride=8), :].astype(BF) for c in range(parts)], axis=1
    )


def regroup_kernel(got_ref, out_ref, wide):
    widen(got_ref, wide)
    for e in range(8):
        out_ref[e] = rows_of(wide, e)


def spread(values, e, wide):
    parts, n, _ = wide.shape
    for c in range(parts):
        wide[c, pl.ds(e, n // 8, stride=8), :] = values[:, c * 128 : (c + 1) * 128]


def narrow(wide, out_ref):
    for c in range(wide.shape[0]):
        out_ref[:, c * 128 : (c + 1) * 128] = wide[c].astype(BF)


def there_kernel(got_ref, a_ref, b_ref, freq_ref, spec_ref, out0_ref, out1_ref, wide, back0, back1):
    step, each = pl.program_id(0), freq_ref.shape[0]

    @pl.when(step == 0)
    def _():
        widen(got_ref, wide)

    m = b_ref.shape[0] // 2
    for j in range(each):
        e = step * each + j
        values = dot(a_ref[...], rows_of(wide, e))
        spec_ref[j] = values
        result = dot(b_ref[...], (values * freq_ref[j].astype(F32)).astype(BF))
        spread(result[:m], e, back0)
        spread(result[m:], e, back1)

    @pl.when(step == 8 // each - 1)
    def _():
        narrow(back0, out0_ref)
        narrow(back1, out1_ref)


def back_kernel(first_ref, got_ref, a_ref, b_ref, freq_ref, spec_ref, grad_ref, out_ref, wide, back):
    step, each = pl.program_id(0), freq_ref.shape[0]

    @pl.when(step == 0)
    def _():
        widen(got_ref, wide)

    m = a_ref.shape[1] // 2
    for j in range(each):
        e = step * each + j
        values = dot(a_ref[:, :m], first_ref[j]) + dot(a_ref[:, m:], rows_of(wide, e))
        grad_ref[j] = values * spec_ref[j]
        spread(dot(b_ref[...], (values * freq_ref[j].astype(F32)).astype(BF)), e, back)

    @pl.when(step == 8 // each - 1)
    def _():
        narrow(back, out_ref)


def front_kernel(got_ref, mat_ref, x_ref, gate_w_ref, first_t_ref,
                 conv_ref, gate_ref, mixed_ref, s0_ref, s1_ref, s2_ref, s3_ref, parts):
    t = pl.program_id(0)
    n = mat_ref.shape[1]
    piece = s0_ref.shape[0]

    @pl.when(t == 0)
    def _():
        for i, part in enumerate(separate(got_ref[...], 2)):
            parts[i * n : (i + 1) * n, :] = part

    conv = dot(mat_ref[...], parts[pl.ds(pl.multiple_of(t * n, n), n), :])
    x = x_ref[...]
    gate = jax.nn.sigmoid(dot(x, gate_w_ref[...]))
    mixed = (x.astype(F32) + gate * conv).astype(BF)
    conv_ref[...] = conv
    gate_ref[...] = gate
    mixed_ref[...] = mixed
    first = dot(first_t_ref[...], mixed, ((1,), (1,))).astype(BF)
    for k, send in enumerate((s0_ref, s1_ref, s2_ref, s3_ref)):
        send[...] = first[k * piece : (k + 1) * piece, :]


def middle_kernel(*refs):
    shuf, up = refs[:4], refs[4:8]
    w_ref, wt_ref = refs[8:10]
    all_ref, gso_ref = refs[10:12]
    merged, back = refs[12:16], refs[16:20]
    piece = shuf[0].shape[0]
    xs = jnp.concatenate([r[...] for r in shuf], axis=0)
    ups = jnp.concatenate([r[...] for r in up], axis=0)
    all_ref[...] = xs
    out = dot(wt_ref[...], xs).astype(BF)
    m = out.astype(F32)
    slope = 0.5 * (1.0 + lax.erf(m * ROOT_HALF)) + m * (INV_ROOT_2PI * jnp.exp(-0.5 * m * m))
    gso = (ups.astype(F32) * slope).astype(BF)
    gso_ref[...] = gso
    gsh = dot(w_ref[...], gso).astype(BF)
    for k in range(4):
        merged[k][...] = out[k * piece : (k + 1) * piece, :]
        back[k][...] = gsh[k * piece : (k + 1) * piece, :]


def rear_kernel(g0_ref, g1_ref, g2_ref, g3_ref, first_t_ref, up_ref, gate_ref, conv_ref, mat_ref,
                gate_w_ref, out_ref, base_ref, ggp_ref, gfo_ref, opened_all):
    step = pl.program_id(0)
    n = mat_ref.shape[0]
    rows = up_ref.shape[0]
    gfo = jnp.concatenate([r[...] for r in (g0_ref, g1_ref, g2_ref, g3_ref)], axis=0)
    gfo_ref[...] = gfo
    gm = up_ref[...].astype(F32) + dot(gfo, first_t_ref[...], ((0,), (0,)))
    gate = gate_ref[...]
    opened = gm * gate
    opened_all[pl.ds(pl.multiple_of(step * rows, rows), rows), :] = opened.astype(BF)
    ggp = (opened * conv_ref[...] * (1.0 - gate)).astype(BF)
    ggp_ref[...] = ggp
    base_ref[...] = gm + dot(ggp, gate_w_ref[...], ((1,), (1,)))

    @pl.when(step == 2 * n // rows - 1)
    def _():
        for t in range(0, n, 256):
            part = mat_ref[t : t + 256, :]
            out_ref[2 * t : 2 * (t + 256), :] = interleave(
                [dot(part, opened_all[i * n : (i + 1) * n, :]) for i in range(2)]
            )


def layer_kernel(*refs):
    plain_ref, mixed, blocks, out_ref = refs[0], refs[1:3], (refs[3:7], refs[7:11]), refs[11]
    for i in range(2):

        @pl.when(pl.program_id(0) // 2 == i)
        def _(i=i):
            merged = jnp.concatenate([r[...] for r in blocks[i]], axis=0)
            m = dot(merged, plain_ref[...], ((0,), (0,)))
            gelu = 0.5 * m * (1.0 + lax.erf(m * ROOT_HALF))
            out_ref[...] = (mixed[i][...].astype(F32) + gelu).astype(BF)


def last_kernel(got_ref, mat_ref, base0_ref, base1_ref, out_ref, parts):
    a = pl.program_id(0)
    n = mat_ref.shape[0]

    @pl.when(a == 0)
    def _():
        for i, part in enumerate(separate(got_ref[...], 4)):
            parts[i * n : (i + 1) * n, :] = part

    conv_back = dot(mat_ref[...], parts[pl.ds(pl.multiple_of(a * n, n), n), :])

    @pl.when(a < 2)
    def _():
        out_ref[...] = (base0_ref[...] + conv_back).astype(BF)

    @pl.when(a >= 2)
    def _():
        out_ref[...] = (base1_ref[...] + conv_back).astype(BF)


def turn_kernel(x_ref, plain_ref, *sends):
    piece = sends[0].shape[0]
    turned = dot(plain_ref[...], x_ref[...], ((1,), (1,))).astype(BF)
    for k in range(4):
        sends[k][...] = turned[k * piece : (k + 1) * piece, :]


def prepare_kernel(order_ref, io_ref, plain_ref, block_ref, mix1_ref, mix2_ref,
                   io_out, io_t_out, first_t_out, second_out, second_t_out):
    order = order_ref[...]
    io = dot(io_ref[...], order, ((1,), (1,)))
    io_out[...] = io.astype(BF)
    io_t_out[...] = io.T.astype(BF)
    first_t_out[...] = dot(plain_ref[...], mix1_ref[...], ((1,), (1,))).astype(BF)
    block = block_ref[...]
    second = dot(dot(block, mix2_ref[...]).astype(BF), block, ((1,), (1,)))
    second_out[...] = second.astype(BF)
    second_t_out[...] = second.T.astype(BF)


def thirds(x):
    high = x.astype(BF)
    rest = x - high.astype(F32)
    middle = rest.astype(BF)
    return high, middle, (rest - middle.astype(F32)).astype(BF)


def pack_kernel(s0_ref, s1_ref, s2_ref, pick_ref, pick_plain_ref, pick_block_ref, block_ref,
                *outs, scale):
    s2 = sum(dot(p, block_ref[...]) for p in thirds(s2_ref[...]))
    cut = [thirds(s0_ref[...]), thirds(s1_ref[...]), thirds(s2)]
    w = s0_ref.shape[1]
    n = pick_ref.shape[0] // 4
    for k in range(4):
        parts = [
            (sum(dot(p[k * n : (k + 1) * n, :], x) for x in c) * scale).reshape(n // 8, 8, w)
            for p, c in zip((pick_ref, pick_plain_ref, pick_block_ref), cut)
        ]
        outs[k][...] = jnp.concatenate(parts, axis=1).reshape(3 * n, w)


def add_kernel(a_ref, b_ref, c_ref, d_ref, *outs):
    n = outs[0].shape[0]
    for k, out in enumerate(outs):
        at = slice(k * n, (k + 1) * n)
        out[...] = (a_ref[at, :] + b_ref[at, :]) + (c_ref[at, :] + d_ref[at, :])


def swap(x):
    return lax.all_to_all(x, CTX, 0, 0, tiled=True)


def exchange(blocks, axes=TP):
    return [blocks[0]] + [
        lax.ppermute(blocks[k], axes, [(i, i ^ k) for i in range(4)]) for k in (1, 2, 3)
    ]


def one_hot(rows, columns, match):
    r = lax.broadcasted_iota(jnp.int32, (rows, columns), 0)
    c = lax.broadcasted_iota(jnp.int32, (rows, columns), 1)
    return match(r, c)


def local(
    hidden_in, fac_inner, fac_outer, inv_outer, inv_inner,
    kernel_freq, gate_blocks, mix_first, mix_second, upstream,
):
    rows, width = hidden_in.shape
    inner, outer = fac_inner.shape[0], fac_outer.shape[0]
    ctx = outer // (rows // inner)
    piece = width // 4
    toks = rows // HALVES
    cols = width // ctx
    me = lax.axis_index(TP)
    pair = range(HALVES)

    def shape(*dims, dtype=BF):
        return jax.ShapeDtypeStruct(dims, dtype)

    tall = [columns_at(shape(piece, toks), TILE)] * 4
    sheet = shape(toks, width)
    wide_sheet = shape(toks, width, dtype=F32)
    tiles = toks // TILE

    def plain_of(r):
        return ((r // piece) ^ me) * piece + r % piece

    def block_of(r):
        return (r % piece) * 4 + ((r // piece) ^ me)

    def outer_of(r):
        return (r % (2 * ctx)) // 2 * 4 + r // (2 * ctx) * 2 + r % 2

    def share_of(r):
        near = r // 8
        at = (((near // 16) ^ lax.axis_index("y")) * 4 + ((near // 4 % 4) ^ lax.axis_index("x"))) * 4
        at = at + ((near % 4) ^ lax.axis_index("z_lo"))
        return jnp.where(r % 8 < cols, at * cols + r % 8, -1)

    plain = one_hot(width, width, lambda r, c: plain_of(r) == c).astype(BF)
    block = one_hot(width, width, lambda r, c: block_of(r) == c).astype(BF)
    order = one_hot(outer, outer, lambda r, c: outer_of(r) == c).astype(BF)
    pick = one_hot(ctx * 8, width, lambda r, c: share_of(r) == c).astype(BF)
    pick_plain = one_hot(ctx * 8, width, lambda r, c: share_of(r) == plain_of(c)).astype(BF)
    pick_block = one_hot(ctx * 8, width, lambda r, c: share_of(r) == block_of(c)).astype(BF)

    inner_flops = 2 * rows * width * inner
    sent = call(
        inner_kernel, 4, [whole(hidden_in), columns_at(fac_inner, inner // 4)],
        [rows_at(shape(rows, width), rows // 4)], inner_flops,
    )
    got = swap(sent[0])
    up = [
        exchange(call(
            turn_kernel, tiles, [rows_at(upstream, TILE, i * tiles), whole(plain)], tall,
            2 * toks * width * width, after=sent,
        ))
        for i in pair
    ]
    square = whole(shape(width, width))
    io, io_t, first_t, second, second_t = call(
        prepare_kernel, 1, [whole(m) for m in (order, inv_outer, plain, block, mix_first, mix_second)],
        [whole(shape(outer, outer))] * 2 + [square] * 3, 4 * outer**3 + 6 * width**3, after=sent,
    )
    freq = kernel_freq.transpose(1, 0, 2)
    inv_inner_t = inv_inner.T

    half = outer // 2
    eb = 8
    wide = pltpu.VMEM((width // 128, rows, 128), F32)
    thin = pltpu.VMEM((width // 128, toks, 128), F32)
    spec_flops = 2 * 2 * outer * outer * eb * width
    spectrum, *sent = call(
        there_kernel, 2, [whole(got), whole(fac_outer.T), whole(io_t), rows_at(freq, 4)],
        [rows_at(shape(eb, outer, width, dtype=F32), 4), whole(sheet), whole(sheet)],
        spec_flops, (wide, thin, thin),
        after=(*up[0][2:], up[1][2], first_t, second, second_t, inv_inner_t, pick, pick_plain, pick_block),
    )
    got = [swap(s) for s in sent]

    conv, gate, mixed, shuf = [], [], [], []
    for i in pair:
        c, g, m, *blocks = call(
            front_kernel, tiles,
            [whole(got[i]), whole(inv_inner_t),
             rows_at(hidden_in, TILE, i * tiles), whole(gate_blocks), whole(first_t)],
            [rows_at(wide_sheet, TILE), rows_at(wide_sheet, TILE), rows_at(sheet, TILE)] + tall,
            2 * toks * width * (inner + 2 * width), (pltpu.VMEM((toks, width), BF),),
            after=tuple(shuf[0][2:3]) if shuf else (),
        )
        conv.append(c), gate.append(g), mixed.append(m)
        shuf.append(exchange(blocks))

    bases, got, merged, middle, back = [], [], [], [], []
    sums = [0.0, 0.0, 0.0]
    for i in pair:
        middle.append(call(
            middle_kernel, tiles,
            [columns_at(b, TILE) for b in (*shuf[i], *up[i])] + [whole(second), whole(second_t)],
            [columns_at(shape(width, toks), TILE)] * 2 + tall * 2, 2 * toks * width * 2 * width,
            after=(mixed[1], shuf[1][1]),
        ))
        back.append(exchange(middle[i][6:]))
    for i in pair:
        shuf_all, gso, *blocks = middle[i]
        sent, base, ggp, gfo = call(
            rear_kernel, tiles,
            [columns_at(b, TILE) for b in back[i]]
            + [whole(first_t), rows_at(upstream, TILE, i * tiles), rows_at(gate[i], TILE),
               rows_at(conv[i], TILE), whole(inv_inner), whole(gate_blocks)],
            [whole(sheet), rows_at(wide_sheet, TILE), rows_at(sheet, TILE),
             columns_at(shape(width, toks), TILE)],
            2 * toks * width * (inner + width), (pltpu.VMEM((toks, width), BF),),
            after=(middle[1][1],),
        )
        merged.append(exchange(blocks[:4]))
        got.append(swap(sent))
        bases.append(base)
        sums[0] += dot(ggp, hidden_in[i * toks : (i + 1) * toks], ((0,), (0,)))
        sums[1] += dot(gfo, mixed[i])
        sums[2] += dot(gso, shuf_all, ((1,), (1,)))

    shares = ctx * 24
    near = []

    def share(n):
        return whole(shape(n, width, dtype=F32))

    parts = call(
        functools.partial(pack_kernel, scale=1.0 / math.sqrt(rows * ctx)), 1,
        [whole(m) for m in (*sums, pick, pick_plain, pick_block, block)], [share(shares // 4)] * 4,
        18 * shares * width * width,
    )
    near.append(exchange(parts, "y"))

    first, = call(
        regroup_kernel, 1, [whole(got[0])], [whole(shape(eb, half, width))], 0, (thin,),
    )
    grad_kernel, sent = call(
        back_kernel, 2,
        [rows_at(first, 4), whole(got[1]), whole(io), whole(fac_outer), rows_at(freq, 4), rows_at(spectrum, 4)],
        [rows_at(shape(eb, outer, width, dtype=F32), 4), whole(shape(rows, width))],
        spec_flops, (thin, wide), after=(parts[0], merged[0][2]),
    )
    got = swap(sent)
    grad_kernel = grad_kernel.transpose(1, 0, 2)
    for axis, n, late in (("x", shares // 16, merged[0][3]), ("z_lo", shares // 64, merged[1][2])):
        parts = call(add_kernel, 1, [whole(p) for p in near[-1]], [share(n)] * 4, 0, after=(late,))
        near.append(exchange(parts, axis))
    total, = call(
        add_kernel, 1, [whole(p) for p in near[2]], [share(24)], 0, after=(merged[1][3],)
    )
    total = [total[8 * i : 8 * i + cols].T for i in range(3)]
    early = lambda a: (0, jnp.minimum(a, 1))
    late = lambda a: (0, jnp.maximum(a - 2, 0))
    layer_out, = call(
        layer_kernel, 4,
        [whole(plain), (mixed[0], (TILE, width), lambda a: (jnp.minimum(a, 1), 0)),
         (mixed[1], (TILE, width), lambda a: (jnp.maximum(a - 2, 0), 0))]
        + [(b, (piece, TILE), early) for b in merged[0]] + [(b, (piece, TILE), late) for b in merged[1]],
        [rows_at(shape(rows, width), TILE)], 2 * rows * width * width, after=tuple(total),
    )
    grad_input, = call(
        last_kernel, 4,
        [whole(got), whole(fac_inner), (bases[0], (inner, width), lambda a: (jnp.minimum(a, 1), 0)),
         (bases[1], (inner, width), lambda a: (jnp.maximum(a - 2, 0), 0))],
        [rows_at(shape(rows, width), inner)], inner_flops, (pltpu.VMEM((rows, width), BF),),
        after=(grad_kernel, *total),
    )
    return (layer_out, grad_input, grad_kernel, *total)


def solution(mesh):
    fine = Mesh(mesh.devices.reshape(4, 4, 4, 2, 2), CTX + TP)
    tok = P(CTX, TP)
    mat = P(TP, None)
    small = P(TP, CTX)
    freq = P(None, CTX, TP)
    return jax.shard_map(
        local,
        mesh=fine,
        in_specs=(tok, P(), P(), P(), P(), freq, mat, mat, mat, tok),
        out_specs=(tok, tok, freq, small, small, small),
        check_vma=False,
    )
```

```python
import functools
import math

import jax
import jax.numpy as jnp
from jax import lax
from jax.experimental import pallas as pl
from jax.experimental.pallas import tpu as pltpu
from jax.sharding import Mesh
from jax.sharding import PartitionSpec as P

CTX = ("y", "x", "z_lo")
TP = ("z_hi", "core")
HALVES = 2
BF = jnp.bfloat16
F32 = jnp.float32
TILE = 512
VMEM_LIMIT = 64 * 1024 * 1024
ROOT_HALF = math.sqrt(0.5)
INV_ROOT_2PI = 1.0 / math.sqrt(2.0 * math.pi)


def dot(left, right, dims=((1,), (0,)), precision=None):
    return lax.dot_general(
        left, right, (dims, ((), ())), precision=precision, preferred_element_type=F32
    )


def whole(array):
    return array, array.shape, lambda g: (0,) * len(array.shape)


def rows_at(array, n, start=0):
    return array, (n,) + array.shape[1:], lambda g: (start + g,) + (0,) * (len(array.shape) - 1)


def columns_at(array, n):
    return array, (array.shape[0], n), lambda g: (0, g)


def call(body, steps, args, outs, flops, scratch=(), after=()):
    arrays = [a[0] for a in args]
    n, late = len(args), len(after)

    def wrapped(*refs):
        body(*refs[:n], *refs[n + late :])

    moved = sum(math.prod(a.shape) * jnp.dtype(a.dtype).itemsize for a in arrays + [o[0] for o in outs])
    return pl.pallas_call(
        wrapped,
        grid=(steps,),
        out_shape=[o[0] for o in outs],
        in_specs=[pl.BlockSpec(a[1], a[2]) for a in args] + [pl.BlockSpec(memory_space=pl.ANY)] * late,
        out_specs=[pl.BlockSpec(o[1], o[2]) for o in outs],
        scratch_shapes=list(scratch),
        compiler_params=pltpu.CompilerParams(vmem_limit_bytes=VMEM_LIMIT),
        cost_estimate=pl.CostEstimate(
            flops=int(flops), bytes_accessed=int(moved), transcendentals=0
        ),
    )(*arrays, *after)


def interleave(parts):
    n, w = parts[0].shape
    cut = [p.reshape(n // 8, 1, 8, w) for p in parts]
    return jnp.concatenate(cut, axis=1).reshape(len(parts) * n, w).astype(BF)


def separate(rows, k):
    n, w = rows.shape
    cut = rows.astype(F32).reshape(n // (8 * k), k, 8, w)
    return [cut[:, i].reshape(n // k, w).astype(BF) for i in range(k)]


def inner_kernel(x_ref, mat_ref, out_ref):
    n = mat_ref.shape[0]
    part = mat_ref[...]
    blocks = [x_ref[i * n : (i + 1) * n, :] for i in range(x_ref.shape[0] // n)]
    out_ref[...] = interleave([dot(part, x, ((0,), (0,))) for x in blocks])


def widen(got_ref, wide):
    for c in range(wide.shape[0]):
        wide[c] = got_ref[:, c * 128 : (c + 1) * 128].astype(F32)


def rows_of(wide, e):
    parts, n, _ = wide.shape
    return jnp.concatenate(
        [wide[c, pl.ds(e, n // 8, stride=8), :].astype(BF) for c in range(parts)], axis=1
    )


def regroup_kernel(got_ref, out_ref, wide):
    widen(got_ref, wide)
    for e in range(8):
        out_ref[e] = rows_of(wide, e)


def spread(values, e, wide):
    parts, n, _ = wide.shape
    for c in range(parts):
        wide[c, pl.ds(e, n // 8, stride=8), :] = values[:, c * 128 : (c + 1) * 128]


def narrow(wide, out_ref):
    for c in range(wide.shape[0]):
        out_ref[:, c * 128 : (c + 1) * 128] = wide[c].astype(BF)


def there_kernel(got_ref, a_ref, b_ref, freq_ref, spec_ref, out0_ref, out1_ref, wide, back0, back1):
    step, each = pl.program_id(0), freq_ref.shape[0]

    @pl.when(step == 0)
    def _():
        widen(got_ref, wide)

    m = b_ref.shape[0] // 2
    for j in range(each):
        e = step * each + j
        values = dot(a_ref[...], rows_of(wide, e))
        spec_ref[j] = values
        result = dot(b_ref[...], (values * freq_ref[j].astype(F32)).astype(BF))
        spread(result[:m], e, back0)
        spread(result[m:], e, back1)

    @pl.when(step == 8 // each - 1)
    def _():
        narrow(back0, out0_ref)
        narrow(back1, out1_ref)


def back_kernel(first_ref, got_ref, a_ref, b_ref, freq_ref, spec_ref, grad_ref, out_ref, wide, back):
    step, each = pl.program_id(0), freq_ref.shape[0]

    @pl.when(step == 0)
    def _():
        widen(got_ref, wide)

    m = a_ref.shape[1] // 2
    for j in range(each):
        e = step * each + j
        values = dot(a_ref[:, :m], first_ref[j]) + dot(a_ref[:, m:], rows_of(wide, e))
        grad_ref[j] = values * spec_ref[j]
        spread(dot(b_ref[...], (values * freq_ref[j].astype(F32)).astype(BF)), e, back)

    @pl.when(step == 8 // each - 1)
    def _():
        narrow(back, out_ref)


def front_kernel(got_ref, mat_ref, x_ref, gate_w_ref, first_t_ref,
                 conv_ref, gate_ref, mixed_ref, s0_ref, s1_ref, s2_ref, s3_ref, parts):
    t = pl.program_id(0)
    n = mat_ref.shape[1]
    piece = s0_ref.shape[0]

    @pl.when(t == 0)
    def _():
        for i, part in enumerate(separate(got_ref[...], 2)):
            parts[i * n : (i + 1) * n, :] = part

    conv = dot(mat_ref[...], parts[pl.ds(pl.multiple_of(t * n, n), n), :])
    x = x_ref[...]
    gate = jax.nn.sigmoid(dot(x, gate_w_ref[...]))
    mixed = (x.astype(F32) + gate * conv).astype(BF)
    conv_ref[...] = conv
    gate_ref[...] = gate
    mixed_ref[...] = mixed
    first = dot(first_t_ref[...], mixed, ((1,), (1,))).astype(BF)
    for k, send in enumerate((s0_ref, s1_ref, s2_ref, s3_ref)):
        send[...] = first[k * piece : (k + 1) * piece, :]


def middle_kernel(*refs):
    shuf, up = refs[:4], refs[4:8]
    w_ref, wt_ref = refs[8:10]
    all_ref, gso_ref = refs[10:12]
    merged, back = refs[12:16], refs[16:20]
    piece = shuf[0].shape[0]
    xs = jnp.concatenate([r[...] for r in shuf], axis=0)
    ups = jnp.concatenate([r[...] for r in up], axis=0)
    all_ref[...] = xs
    out = dot(wt_ref[...], xs).astype(BF)
    m = out.astype(F32)
    slope = 0.5 * (1.0 + lax.erf(m * ROOT_HALF)) + m * (INV_ROOT_2PI * jnp.exp(-0.5 * m * m))
    gso = (ups.astype(F32) * slope).astype(BF)
    gso_ref[...] = gso
    gsh = dot(w_ref[...], gso).astype(BF)
    for k in range(4):
        merged[k][...] = out[k * piece : (k + 1) * piece, :]
        back[k][...] = gsh[k * piece : (k + 1) * piece, :]


def rear_kernel(g0_ref, g1_ref, g2_ref, g3_ref, first_t_ref, up_ref, gate_ref, conv_ref, mat_ref,
                gate_w_ref, out_ref, base_ref, ggp_ref, gfo_ref, opened_all):
    step = pl.program_id(0)
    n = mat_ref.shape[0]
    rows = up_ref.shape[0]
    gfo = jnp.concatenate([r[...] for r in (g0_ref, g1_ref, g2_ref, g3_ref)], axis=0)
    gfo_ref[...] = gfo
    gm = up_ref[...].astype(F32) + dot(gfo, first_t_ref[...], ((0,), (0,)))
    gate = gate_ref[...]
    opened = gm * gate
    opened_all[pl.ds(pl.multiple_of(step * rows, rows), rows), :] = opened.astype(BF)
    ggp = (opened * conv_ref[...] * (1.0 - gate)).astype(BF)
    ggp_ref[...] = ggp
    base_ref[...] = gm + dot(ggp, gate_w_ref[...], ((1,), (1,)))

    @pl.when(step == 2 * n // rows - 1)
    def _():
        for t in range(0, n, 256):
            part = mat_ref[t : t + 256, :]
            out_ref[2 * t : 2 * (t + 256), :] = interleave(
                [dot(part, opened_all[i * n : (i + 1) * n, :]) for i in range(2)]
            )


def layer_kernel(*refs):
    plain_ref, mixed, blocks, out_ref = refs[0], refs[1:3], (refs[3:7], refs[7:11]), refs[11]
    for i in range(2):

        @pl.when(pl.program_id(0) // 2 == i)
        def _(i=i):
            merged = jnp.concatenate([r[...] for r in blocks[i]], axis=0)
            m = dot(merged, plain_ref[...], ((0,), (0,)))
            gelu = 0.5 * m * (1.0 + lax.erf(m * ROOT_HALF))
            out_ref[...] = (mixed[i][...].astype(F32) + gelu).astype(BF)


def last_kernel(got_ref, mat_ref, base0_ref, base1_ref, out_ref, parts):
    a = pl.program_id(0)
    n = mat_ref.shape[0]

    @pl.when(a == 0)
    def _():
        for i, part in enumerate(separate(got_ref[...], 4)):
            parts[i * n : (i + 1) * n, :] = part

    conv_back = dot(mat_ref[...], parts[pl.ds(pl.multiple_of(a * n, n), n), :])

    @pl.when(a < 2)
    def _():
        out_ref[...] = (base0_ref[...] + conv_back).astype(BF)

    @pl.when(a >= 2)
    def _():
        out_ref[...] = (base1_ref[...] + conv_back).astype(BF)


def turn_kernel(x_ref, plain_ref, *sends):
    piece = sends[0].shape[0]
    turned = dot(plain_ref[...], x_ref[...], ((1,), (1,))).astype(BF)
    for k in range(4):
        sends[k][...] = turned[k * piece : (k + 1) * piece, :]


def prepare_kernel(order_ref, io_ref, plain_ref, block_ref, mix1_ref, mix2_ref,
                   io_out, io_t_out, first_t_out, second_out, second_t_out):
    order = order_ref[...]
    io = dot(io_ref[...], order, ((1,), (1,)))
    io_out[...] = io.astype(BF)
    io_t_out[...] = io.T.astype(BF)
    first_t_out[...] = dot(plain_ref[...], mix1_ref[...], ((1,), (1,))).astype(BF)
    block = block_ref[...]
    second = dot(dot(block, mix2_ref[...]).astype(BF), block, ((1,), (1,)))
    second_out[...] = second.astype(BF)
    second_t_out[...] = second.T.astype(BF)


def thirds(x):
    high = x.astype(BF)
    rest = x - high.astype(F32)
    middle = rest.astype(BF)
    return high, middle, (rest - middle.astype(F32)).astype(BF)


def pack_kernel(s0_ref, s1_ref, s2_ref, pick_ref, pick_plain_ref, pick_block_ref, block_ref,
                *outs, scale):
    s2 = sum(dot(p, block_ref[...]) for p in thirds(s2_ref[...]))
    cut = [thirds(s0_ref[...]), thirds(s1_ref[...]), thirds(s2)]
    w = s0_ref.shape[1]
    n = pick_ref.shape[0] // 4
    for k in range(4):
        parts = [
            (sum(dot(p[k * n : (k + 1) * n, :], x) for x in c) * scale).reshape(n // 8, 8, w)
            for p, c in zip((pick_ref, pick_plain_ref, pick_block_ref), cut)
        ]
        outs[k][...] = jnp.concatenate(parts, axis=1).reshape(3 * n, w)


def add_kernel(a_ref, b_ref, c_ref, d_ref, *outs):
    n = outs[0].shape[0]
    for k, out in enumerate(outs):
        at = slice(k * n, (k + 1) * n)
        out[...] = (a_ref[at, :] + b_ref[at, :]) + (c_ref[at, :] + d_ref[at, :])


def swap(x):
    return lax.all_to_all(x, CTX, 0, 0, tiled=True)


def exchange(blocks, axes=TP):
    return [blocks[0]] + [
        lax.ppermute(blocks[k], axes, [(i, i ^ k) for i in range(4)]) for k in (1, 2, 3)
    ]


def one_hot(rows, columns, match):
    r = lax.broadcasted_iota(jnp.int32, (rows, columns), 0)
    c = lax.broadcasted_iota(jnp.int32, (rows, columns), 1)
    return match(r, c)


def local(
    hidden_in, fac_inner, fac_outer, inv_outer, inv_inner,
    kernel_freq, gate_blocks, mix_first, mix_second, upstream,
):
    rows, width = hidden_in.shape
    inner, outer = fac_inner.shape[0], fac_outer.shape[0]
    ctx = outer // (rows // inner)
    piece = width // 4
    toks = rows // HALVES
    cols = width // ctx
    me = lax.axis_index(TP)
    pair = range(HALVES)

    def shape(*dims, dtype=BF):
        return jax.ShapeDtypeStruct(dims, dtype)

    tall = [columns_at(shape(piece, toks), TILE)] * 4
    sheet = shape(toks, width)
    wide_sheet = shape(toks, width, dtype=F32)
    tiles = toks // TILE

    def plain_of(r):
        return ((r // piece) ^ me) * piece + r % piece

    def block_of(r):
        return (r % piece) * 4 + ((r // piece) ^ me)

    def outer_of(r):
        return (r % (2 * ctx)) // 2 * 4 + r // (2 * ctx) * 2 + r % 2

    def share_of(r):
        near = r // 8
        at = (((near // 16) ^ lax.axis_index("y")) * 4 + ((near // 4 % 4) ^ lax.axis_index("x"))) * 4
        at = at + ((near % 4) ^ lax.axis_index("z_lo"))
        return jnp.where(r % 8 < cols, at * cols + r % 8, -1)

    plain = one_hot(width, width, lambda r, c: plain_of(r) == c).astype(BF)
    block = one_hot(width, width, lambda r, c: block_of(r) == c).astype(BF)
    order = one_hot(outer, outer, lambda r, c: outer_of(r) == c).astype(BF)
    pick = one_hot(ctx * 8, width, lambda r, c: share_of(r) == c).astype(BF)
    pick_plain = one_hot(ctx * 8, width, lambda r, c: share_of(r) == plain_of(c)).astype(BF)
    pick_block = one_hot(ctx * 8, width, lambda r, c: share_of(r) == block_of(c)).astype(BF)

    inner_flops = 2 * rows * width * inner
    sent = call(
        inner_kernel, 2, [whole(hidden_in), columns_at(fac_inner, inner // 2)],
        [rows_at(shape(rows, width), rows // 2)], inner_flops,
    )
    got = swap(sent[0])
    up = [
        exchange(call(
            turn_kernel, tiles, [rows_at(upstream, TILE, i * tiles), whole(plain)], tall,
            2 * toks * width * width, after=sent,
        ))
        for i in pair
    ]
    square = whole(shape(width, width))
    io, io_t, first_t, second, second_t = call(
        prepare_kernel, 1, [whole(m) for m in (order, inv_outer, plain, block, mix_first, mix_second)],
        [whole(shape(outer, outer))] * 2 + [square] * 3, 4 * outer**3 + 6 * width**3, after=sent,
    )
    freq = kernel_freq.transpose(1, 0, 2)
    inv_inner_t = inv_inner.T

    half = outer // 2
    eb = 8
    wide = pltpu.VMEM((width // 128, rows, 128), F32)
    thin = pltpu.VMEM((width // 128, toks, 128), F32)
    spec_flops = 2 * 2 * outer * outer * eb * width
    spectrum, *sent = call(
        there_kernel, 2, [whole(got), whole(fac_outer.T), whole(io_t), rows_at(freq, 4)],
        [rows_at(shape(eb, outer, width, dtype=F32), 4), whole(sheet), whole(sheet)],
        spec_flops, (wide, thin, thin),
        after=(*up[0][2:], up[1][2], first_t, second, second_t, inv_inner_t, pick, pick_plain, pick_block),
    )
    got = [swap(s) for s in sent]

    def front(i, after=()):
        return call(
            front_kernel, tiles,
            [whole(got[i]), whole(inv_inner_t), rows_at(hidden_in, TILE, i * tiles), whole(gate_blocks),
             whole(first_t)],
            [rows_at(wide_sheet, TILE), rows_at(wide_sheet, TILE), rows_at(sheet, TILE)] + tall,
            2 * toks * width * (inner + 2 * width), (pltpu.VMEM((toks, width), BF),), after,
        )

    def middle(i, shuf, after=()):
        return call(
            middle_kernel, tiles,
            [columns_at(b, TILE) for b in (*shuf, *up[i])] + [whole(second), whole(second_t)],
            [columns_at(shape(width, toks), TILE)] * 2 + tall * 2, 2 * toks * width * 2 * width,
            (), after,
        )

    def rear(i, back, gate, conv, after=()):
        return call(
            rear_kernel, tiles,
            [columns_at(b, TILE) for b in back]
            + [whole(first_t), rows_at(upstream, TILE, i * tiles), rows_at(gate, TILE),
               rows_at(conv, TILE), whole(inv_inner), whole(gate_blocks)],
            [whole(sheet), rows_at(wide_sheet, TILE), rows_at(sheet, TILE),
             columns_at(shape(width, toks), TILE)],
            2 * toks * width * (inner + 2 * width), (pltpu.VMEM((toks, width), BF),), after,
        )

    conv0, gate0, mixed0, *blocks = front(0)
    shuf0 = exchange(blocks)
    all0, gso0, *blocks0 = middle(0, shuf0)
    back0 = exchange(blocks0[4:])
    conv1, gate1, mixed1, *blocks = front(1, (gso0, back0[1], up[1][1], up[1][3]))
    shuf1 = exchange(blocks)
    sent0, base0, ggp0, gfo0 = rear(0, back0, gate0, conv0, tuple(shuf1[1:]))
    got = [swap(sent0)]
    merged0 = exchange(blocks0[:4])
    all1, gso1, *blocks1 = middle(1, shuf1, (sent0,))
    back1 = exchange(blocks1[4:])
    merged1 = exchange(blocks1[:4])
    sent1, base1, ggp1, gfo1 = rear(1, back1, gate1, conv1)
    got.append(swap(sent1))
    x0, x1 = hidden_in[:toks], hidden_in[toks:]
    sums = (
        dot(ggp0, x0, ((0,), (0,))) + dot(ggp1, x1, ((0,), (0,))),
        dot(gfo0, mixed0) + dot(gfo1, mixed1),
        dot(gso0, all0, ((1,), (1,))) + dot(gso1, all1, ((1,), (1,))),
    )

    shares = ctx * 24
    near = []

    def share(n):
        return whole(shape(n, width, dtype=F32))

    parts = call(
        functools.partial(pack_kernel, scale=1.0 / math.sqrt(rows * ctx)), 1,
        [whole(m) for m in (*sums, pick, pick_plain, pick_block, block)], [share(shares // 4)] * 4,
        18 * shares * width * width, after=tuple(merged0[2:]),
    )
    near.append(exchange(parts, "y"))

    first, = call(
        regroup_kernel, 1, [whole(got[0])], [whole(shape(eb, half, width))], 0, (thin,),
    )
    grad_kernel, sent = call(
        back_kernel, 2,
        [rows_at(first, 4), whole(got[1]), whole(io), whole(fac_outer), rows_at(freq, 4), rows_at(spectrum, 4)],
        [rows_at(shape(eb, outer, width, dtype=F32), 4), whole(shape(rows, width))],
        spec_flops, (thin, wide), after=(parts[0], merged1[2]),
    )
    got = swap(sent)
    grad_kernel = grad_kernel.transpose(1, 0, 2)
    for axis, n in (("x", shares // 16), ("z_lo", shares // 64)):
        parts = call(add_kernel, 1, [whole(p) for p in near[-1]], [share(n)] * 4, 0)
        near.append(exchange(parts, axis))
    total, = call(add_kernel, 1, [whole(p) for p in near[2]], [share(24)], 0)
    total = [total[8 * i : 8 * i + cols].T for i in range(3)]
    early = lambda a: (0, jnp.minimum(a, 1))
    late = lambda a: (0, jnp.maximum(a - 2, 0))
    layer_out, = call(
        layer_kernel, 4,
        [whole(plain), (mixed0, (TILE, width), lambda a: (jnp.minimum(a, 1), 0)),
         (mixed1, (TILE, width), lambda a: (jnp.maximum(a - 2, 0), 0))]
        + [(b, (piece, TILE), early) for b in merged0] + [(b, (piece, TILE), late) for b in merged1],
        [rows_at(shape(rows, width), TILE)], 2 * rows * width * width, after=tuple(total),
    )
    grad_input, = call(
        last_kernel, 4,
        [whole(got), whole(fac_inner), (base0, (inner, width), lambda a: (jnp.minimum(a, 1), 0)),
         (base1, (inner, width), lambda a: (jnp.maximum(a - 2, 0), 0))],
        [rows_at(shape(rows, width), inner)], inner_flops, (pltpu.VMEM((rows, width), BF),),
        after=(grad_kernel, *total),
    )
    return (layer_out, grad_input, grad_kernel, *total)


def solution(mesh):
    fine = Mesh(mesh.devices.reshape(4, 4, 4, 2, 2), CTX + TP)
    tok = P(CTX, TP)
    mat = P(TP, None)
    small = P(TP, CTX)
    freq = P(None, CTX, TP)
    return jax.shard_map(
        local,
        mesh=fine,
        in_specs=(tok, P(), P(), P(), P(), freq, mat, mat, mat, tok),
        out_specs=(tok, tok, freq, small, small, small),
        check_vma=False,
    )
```

```python
import functools
import math

import jax
import jax.numpy as jnp
from jax import lax
from jax.experimental import pallas as pl
from jax.experimental.pallas import tpu as pltpu
from jax.sharding import Mesh
from jax.sharding import PartitionSpec as P

CTX = ("y", "x", "z_lo")
TP = ("z_hi", "core")
HALVES = 2
BF = jnp.bfloat16
F32 = jnp.float32
TILE = 512
VMEM_LIMIT = 64 * 1024 * 1024
ROOT_HALF = math.sqrt(0.5)
INV_ROOT_2PI = 1.0 / math.sqrt(2.0 * math.pi)


def dot(left, right, dims=((1,), (0,)), precision=None):
    return lax.dot_general(
        left, right, (dims, ((), ())), precision=precision, preferred_element_type=F32
    )


def whole(array):
    return array, array.shape, lambda g: (0,) * len(array.shape)


def rows_at(array, n, start=0):
    return array, (n,) + array.shape[1:], lambda g: (start + g,) + (0,) * (len(array.shape) - 1)


def columns_at(array, n):
    return array, (array.shape[0], n), lambda g: (0, g)


def call(body, steps, args, outs, flops, scratch=(), after=()):
    arrays = [a[0] for a in args]
    n, late = len(args), len(after)

    def wrapped(*refs):
        body(*refs[:n], *refs[n + late :])

    moved = sum(math.prod(a.shape) * jnp.dtype(a.dtype).itemsize for a in arrays + [o[0] for o in outs])
    return pl.pallas_call(
        wrapped,
        grid=(steps,),
        out_shape=[o[0] for o in outs],
        in_specs=[pl.BlockSpec(a[1], a[2]) for a in args] + [pl.BlockSpec(memory_space=pl.ANY)] * late,
        out_specs=[pl.BlockSpec(o[1], o[2]) for o in outs],
        scratch_shapes=list(scratch),
        compiler_params=pltpu.CompilerParams(vmem_limit_bytes=VMEM_LIMIT),
        cost_estimate=pl.CostEstimate(
            flops=int(flops), bytes_accessed=int(moved), transcendentals=0
        ),
    )(*arrays, *after)


def interleave(parts):
    n, w = parts[0].shape
    cut = [p.reshape(n // 8, 1, 8, w) for p in parts]
    return jnp.concatenate(cut, axis=1).reshape(len(parts) * n, w).astype(BF)


def separate(rows, k):
    n, w = rows.shape
    cut = rows.astype(F32).reshape(n // (8 * k), k, 8, w)
    return [cut[:, i].reshape(n // k, w).astype(BF) for i in range(k)]


def inner_kernel(x_ref, mat_ref, out_ref):
    n = mat_ref.shape[0]
    part = mat_ref[...]
    blocks = [x_ref[i * n : (i + 1) * n, :] for i in range(x_ref.shape[0] // n)]
    out_ref[...] = interleave([dot(part, x, ((0,), (0,))) for x in blocks])


def widen(got_ref, wide):
    for c in range(wide.shape[0]):
        wide[c] = got_ref[:, c * 128 : (c + 1) * 128].astype(F32)


def rows_of(wide, e):
    parts, n, _ = wide.shape
    return jnp.concatenate(
        [wide[c, pl.ds(e, n // 8, stride=8), :].astype(BF) for c in range(parts)], axis=1
    )


def regroup_kernel(got_ref, out_ref, wide):
    widen(got_ref, wide)
    for e in range(8):
        out_ref[e] = rows_of(wide, e)


def spread(values, e, wide):
    parts, n, _ = wide.shape
    for c in range(parts):
        wide[c, pl.ds(e, n // 8, stride=8), :] = values[:, c * 128 : (c + 1) * 128]


def narrow(wide, out_ref):
    for c in range(wide.shape[0]):
        out_ref[:, c * 128 : (c + 1) * 128] = wide[c].astype(BF)


def there_kernel(got_ref, a_ref, b_ref, freq_ref, spec_ref, out0_ref, out1_ref, wide, back0, back1):
    step, each = pl.program_id(0), freq_ref.shape[0]

    @pl.when(step == 0)
    def _():
        widen(got_ref, wide)

    m = b_ref.shape[0] // 2
    for j in range(each):
        e = step * each + j
        values = dot(a_ref[...], rows_of(wide, e))
        spec_ref[j] = values
        result = dot(b_ref[...], (values * freq_ref[j].astype(F32)).astype(BF))
        spread(result[:m], e, back0)
        spread(result[m:], e, back1)

    @pl.when(step == 8 // each - 1)
    def _():
        narrow(back0, out0_ref)
        narrow(back1, out1_ref)


def back_kernel(first_ref, got_ref, a_ref, b_ref, freq_ref, spec_ref, grad_ref, out_ref, wide, back):
    step, each = pl.program_id(0), freq_ref.shape[0]

    @pl.when(step == 0)
    def _():
        widen(got_ref, wide)

    m = a_ref.shape[1] // 2
    for j in range(each):
        e = step * each + j
        values = dot(a_ref[:, :m], first_ref[j]) + dot(a_ref[:, m:], rows_of(wide, e))
        grad_ref[j] = values * spec_ref[j]
        spread(dot(b_ref[...], (values * freq_ref[j].astype(F32)).astype(BF)), e, back)

    @pl.when(step == 8 // each - 1)
    def _():
        narrow(back, out_ref)


def front_kernel(got_ref, mat_ref, x_ref, gate_w_ref, first_t_ref,
                 conv_ref, gate_ref, mixed_ref, s0_ref, s1_ref, s2_ref, s3_ref, parts):
    t = pl.program_id(0)
    n = mat_ref.shape[1]
    piece = s0_ref.shape[0]

    @pl.when(t == 0)
    def _():
        for i, part in enumerate(separate(got_ref[...], 2)):
            parts[i * n : (i + 1) * n, :] = part

    conv = dot(mat_ref[...], parts[pl.ds(pl.multiple_of(t * n, n), n), :])
    x = x_ref[...]
    gate = jax.nn.sigmoid(dot(x, gate_w_ref[...]))
    mixed = (x.astype(F32) + gate * conv).astype(BF)
    conv_ref[...] = conv
    gate_ref[...] = gate
    mixed_ref[...] = mixed
    first = dot(first_t_ref[...], mixed, ((1,), (1,))).astype(BF)
    for k, send in enumerate((s0_ref, s1_ref, s2_ref, s3_ref)):
        send[...] = first[k * piece : (k + 1) * piece, :]


def middle_kernel(*refs):
    shuf, up = refs[:4], refs[4:8]
    w_ref, wt_ref = refs[8:10]
    all_ref, gso_ref = refs[10:12]
    merged, back = refs[12:16], refs[16:20]
    piece = shuf[0].shape[0]
    xs = jnp.concatenate([r[...] for r in shuf], axis=0)
    ups = jnp.concatenate([r[...] for r in up], axis=0)
    all_ref[...] = xs
    out = dot(wt_ref[...], xs).astype(BF)
    m = out.astype(F32)
    slope = 0.5 * (1.0 + lax.erf(m * ROOT_HALF)) + m * (INV_ROOT_2PI * jnp.exp(-0.5 * m * m))
    gso = (ups.astype(F32) * slope).astype(BF)
    gso_ref[...] = gso
    gsh = dot(w_ref[...], gso).astype(BF)
    for k in range(4):
        merged[k][...] = out[k * piece : (k + 1) * piece, :]
        back[k][...] = gsh[k * piece : (k + 1) * piece, :]


def rear_kernel(g0_ref, g1_ref, g2_ref, g3_ref, first_t_ref, up_ref, gate_ref, conv_ref, mat_ref,
                gate_w_ref, out_ref, base_ref, ggp_ref, gfo_ref, opened_all):
    step = pl.program_id(0)
    n = mat_ref.shape[0]
    rows = up_ref.shape[0]
    gfo = jnp.concatenate([r[...] for r in (g0_ref, g1_ref, g2_ref, g3_ref)], axis=0)
    gfo_ref[...] = gfo
    gm = up_ref[...].astype(F32) + dot(gfo, first_t_ref[...], ((0,), (0,)))
    gate = gate_ref[...]
    opened = gm * gate
    opened_all[pl.ds(pl.multiple_of(step * rows, rows), rows), :] = opened.astype(BF)
    ggp = (opened * conv_ref[...] * (1.0 - gate)).astype(BF)
    ggp_ref[...] = ggp
    base_ref[...] = gm + dot(ggp, gate_w_ref[...], ((1,), (1,)))

    @pl.when(step == 2 * n // rows - 1)
    def _():
        for t in range(0, n, 256):
            part = mat_ref[t : t + 256, :]
            out_ref[2 * t : 2 * (t + 256), :] = interleave(
                [dot(part, opened_all[i * n : (i + 1) * n, :]) for i in range(2)]
            )


def layer_kernel(*refs):
    plain_ref, mixed, blocks, out_ref = refs[0], refs[1:3], (refs[3:7], refs[7:11]), refs[11]
    for i in range(2):

        @pl.when(pl.program_id(0) // 2 == i)
        def _(i=i):
            merged = jnp.concatenate([r[...] for r in blocks[i]], axis=0)
            m = dot(merged, plain_ref[...], ((0,), (0,)))
            gelu = 0.5 * m * (1.0 + lax.erf(m * ROOT_HALF))
            out_ref[...] = (mixed[i][...].astype(F32) + gelu).astype(BF)


def last_kernel(got_ref, mat_ref, base0_ref, base1_ref, out_ref, parts):
    a = pl.program_id(0)
    n = mat_ref.shape[0]

    @pl.when(a == 0)
    def _():
        for i, part in enumerate(separate(got_ref[...], 4)):
            parts[i * n : (i + 1) * n, :] = part

    conv_back = dot(mat_ref[...], parts[pl.ds(pl.multiple_of(a * n, n), n), :])

    @pl.when(a < 2)
    def _():
        out_ref[...] = (base0_ref[...] + conv_back).astype(BF)

    @pl.when(a >= 2)
    def _():
        out_ref[...] = (base1_ref[...] + conv_back).astype(BF)


def turn_kernel(x_ref, plain_ref, *sends):
    piece = sends[0].shape[0]
    turned = dot(plain_ref[...], x_ref[...], ((1,), (1,))).astype(BF)
    for k in range(4):
        sends[k][...] = turned[k * piece : (k + 1) * piece, :]


def prepare_kernel(order_ref, io_ref, plain_ref, block_ref, mix1_ref, mix2_ref,
                   io_out, io_t_out, first_t_out, second_out, second_t_out):
    order = order_ref[...]
    io = dot(io_ref[...], order, ((1,), (1,)))
    io_out[...] = io.astype(BF)
    io_t_out[...] = io.T.astype(BF)
    first_t_out[...] = dot(plain_ref[...], mix1_ref[...], ((1,), (1,))).astype(BF)
    block = block_ref[...]
    second = dot(dot(block, mix2_ref[...]).astype(BF), block, ((1,), (1,)))
    second_out[...] = second.astype(BF)
    second_t_out[...] = second.T.astype(BF)


def thirds(x):
    high = x.astype(BF)
    rest = x - high.astype(F32)
    middle = rest.astype(BF)
    return high, middle, (rest - middle.astype(F32)).astype(BF)


def pack_kernel(s0_ref, s1_ref, s2_ref, pick_ref, pick_plain_ref, pick_block_ref, block_ref,
                *outs, scale):
    s2 = sum(dot(p, block_ref[...]) for p in thirds(s2_ref[...]))
    cut = [thirds(s0_ref[...]), thirds(s1_ref[...]), thirds(s2)]
    w = s0_ref.shape[1]
    n = pick_ref.shape[0] // 4
    for k in range(4):
        parts = [
            (sum(dot(p[k * n : (k + 1) * n, :], x) for x in c) * scale).reshape(n // 8, 8, w)
            for p, c in zip((pick_ref, pick_plain_ref, pick_block_ref), cut)
        ]
        outs[k][...] = jnp.concatenate(parts, axis=1).reshape(3 * n, w)


def add_kernel(a_ref, b_ref, c_ref, d_ref, *outs):
    n = outs[0].shape[0]
    for k, out in enumerate(outs):
        at = slice(k * n, (k + 1) * n)
        out[...] = (a_ref[at, :] + b_ref[at, :]) + (c_ref[at, :] + d_ref[at, :])


def total_kernel(a_ref, b_ref, c_ref, d_ref, *outs):
    total = (a_ref[...] + b_ref[...]) + (c_ref[...] + d_ref[...])
    for i, out in enumerate(outs):
        out[...] = total[8 * i : 8 * i + 8].T[:, : out.shape[1]]


def swap(x):
    return lax.all_to_all(x, CTX, 0, 0, tiled=True)


def exchange(blocks, axes=TP):
    return [blocks[0]] + [
        lax.ppermute(blocks[k], axes, [(i, i ^ k) for i in range(4)]) for k in (1, 2, 3)
    ]


def one_hot(rows, columns, match):
    r = lax.broadcasted_iota(jnp.int32, (rows, columns), 0)
    c = lax.broadcasted_iota(jnp.int32, (rows, columns), 1)
    return match(r, c)


def local(
    hidden_in, fac_inner, fac_outer, inv_outer, inv_inner,
    kernel_freq, gate_blocks, mix_first, mix_second, upstream,
):
    rows, width = hidden_in.shape
    inner, outer = fac_inner.shape[0], fac_outer.shape[0]
    ctx = outer // (rows // inner)
    piece = width // 4
    toks = rows // HALVES
    cols = width // ctx
    me = lax.axis_index(TP)
    pair = range(HALVES)

    def shape(*dims, dtype=BF):
        return jax.ShapeDtypeStruct(dims, dtype)

    tall = [columns_at(shape(piece, toks), TILE)] * 4
    sheet = shape(toks, width)
    wide_sheet = shape(toks, width, dtype=F32)
    tiles = toks // TILE

    def plain_of(r):
        return ((r // piece) ^ me) * piece + r % piece

    def block_of(r):
        return (r % piece) * 4 + ((r // piece) ^ me)

    def outer_of(r):
        return (r % (2 * ctx)) // 2 * 4 + r // (2 * ctx) * 2 + r % 2

    def share_of(r):
        near = r // 8
        at = (((near // 16) ^ lax.axis_index("y")) * 4 + ((near // 4 % 4) ^ lax.axis_index("x"))) * 4
        at = at + ((near % 4) ^ lax.axis_index("z_lo"))
        return jnp.where(r % 8 < cols, at * cols + r % 8, -1)

    plain = one_hot(width, width, lambda r, c: plain_of(r) == c).astype(BF)
    block = one_hot(width, width, lambda r, c: block_of(r) == c).astype(BF)
    order = one_hot(outer, outer, lambda r, c: outer_of(r) == c).astype(BF)
    pick = one_hot(ctx * 8, width, lambda r, c: share_of(r) == c).astype(BF)
    pick_plain = one_hot(ctx * 8, width, lambda r, c: share_of(r) == plain_of(c)).astype(BF)
    pick_block = one_hot(ctx * 8, width, lambda r, c: share_of(r) == block_of(c)).astype(BF)

    inner_flops = 2 * rows * width * inner
    sent = call(
        inner_kernel, 2, [whole(hidden_in), columns_at(fac_inner, inner // 2)],
        [rows_at(shape(rows, width), rows // 2)], inner_flops,
    )
    got = swap(sent[0])
    up = [
        exchange(call(
            turn_kernel, tiles, [rows_at(upstream, TILE, i * tiles), whole(plain)], tall,
            2 * toks * width * width, after=sent,
        ))
        for i in pair
    ]
    square = whole(shape(width, width))
    io, io_t, first_t, second, second_t = call(
        prepare_kernel, 1, [whole(m) for m in (order, inv_outer, plain, block, mix_first, mix_second)],
        [whole(shape(outer, outer))] * 2 + [square] * 3, 4 * outer**3 + 6 * width**3, after=sent,
    )
    freq = kernel_freq.transpose(1, 0, 2)
    inv_inner_t = inv_inner.T

    half = outer // 2
    eb = 8
    wide = pltpu.VMEM((width // 128, rows, 128), F32)
    thin = pltpu.VMEM((width // 128, toks, 128), F32)
    spec_flops = 2 * 2 * outer * outer * eb * width
    spectrum, *sent = call(
        there_kernel, 2, [whole(got), whole(fac_outer.T), whole(io_t), rows_at(freq, 4)],
        [rows_at(shape(eb, outer, width, dtype=F32), 4), whole(sheet), whole(sheet)],
        spec_flops, (wide, thin, thin),
        after=(*up[0][2:], up[1][2], first_t, second, second_t, inv_inner_t, pick, pick_plain, pick_block),
    )
    got = [swap(s) for s in sent]

    def front(i, after=()):
        return call(
            front_kernel, tiles,
            [whole(got[i]), whole(inv_inner_t), rows_at(hidden_in, TILE, i * tiles), whole(gate_blocks),
             whole(first_t)],
            [rows_at(wide_sheet, TILE), rows_at(wide_sheet, TILE), rows_at(sheet, TILE)] + tall,
            2 * toks * width * (inner + 2 * width), (pltpu.VMEM((toks, width), BF),), after,
        )

    def middle(i, shuf, after=()):
        return call(
            middle_kernel, tiles,
            [columns_at(b, TILE) for b in (*shuf, *up[i])] + [whole(second), whole(second_t)],
            [columns_at(shape(width, toks), TILE)] * 2 + tall * 2, 2 * toks * width * 2 * width,
            (), after,
        )

    def rear(i, back, gate, conv, after=()):
        return call(
            rear_kernel, tiles,
            [columns_at(b, TILE) for b in back]
            + [whole(first_t), rows_at(upstream, TILE, i * tiles), rows_at(gate, TILE),
               rows_at(conv, TILE), whole(inv_inner), whole(gate_blocks)],
            [whole(sheet), rows_at(wide_sheet, TILE), rows_at(sheet, TILE),
             columns_at(shape(width, toks), TILE)],
            2 * toks * width * (inner + 2 * width), (pltpu.VMEM((toks, width), BF),), after,
        )

    conv0, gate0, mixed0, *blocks = front(0)
    shuf0 = exchange(blocks)
    conv1, gate1, mixed1, *blocks = front(1, (shuf0[2],))
    shuf1 = exchange(blocks)
    all0, gso0, *blocks0 = middle(0, shuf0, (mixed1, shuf1[1]))
    back0 = exchange(blocks0[4:])
    all1, gso1, *blocks1 = middle(1, shuf1)
    back1 = exchange(blocks1[4:])
    sent0, base0, ggp0, gfo0 = rear(0, back0, gate0, conv0, (gso1,))
    got = [swap(sent0)]
    merged0 = exchange(blocks0[:4])
    merged1 = exchange(blocks1[:4])
    x0, x1 = hidden_in[:toks], hidden_in[toks:]
    gate_sum = dot(ggp0, x0, ((0,), (0,)))
    first_sum = dot(gfo0, mixed0)
    second_sum = dot(gso0, all0, ((1,), (1,))) + dot(gso1, all1, ((1,), (1,)))
    sent1, base1, ggp1, gfo1 = rear(1, back1, gate1, conv1, (gate_sum, first_sum, second_sum))
    got.append(swap(sent1))
    sums = (
        gate_sum + dot(ggp1, x1, ((0,), (0,))),
        first_sum + dot(gfo1, mixed1),
        second_sum,
    )

    shares = ctx * 24
    near = []

    def share(n):
        return whole(shape(n, width, dtype=F32))

    parts = call(
        functools.partial(pack_kernel, scale=1.0 / math.sqrt(rows * ctx)), 1,
        [whole(m) for m in (*sums, pick, pick_plain, pick_block, block)], [share(shares // 4)] * 4,
        18 * shares * width * width, after=tuple(merged0[2:]),
    )
    near.append(exchange(parts, "y"))

    first, = call(
        regroup_kernel, 1, [whole(got[0])], [whole(shape(eb, half, width))], 0, (thin,),
    )
    grad_kernel, sent = call(
        back_kernel, 2,
        [rows_at(first, 4), whole(got[1]), whole(io), whole(fac_outer), rows_at(freq, 4), rows_at(spectrum, 4)],
        [rows_at(shape(eb, outer, width, dtype=F32), 4), whole(shape(rows, width))],
        spec_flops, (thin, wide), after=(*near[0][1:], *merged1[2:]),
    )
    got = swap(sent)
    grad_kernel = grad_kernel.transpose(1, 0, 2)
    for axis, n in (("x", shares // 16), ("z_lo", shares // 64)):
        parts = call(add_kernel, 1, [whole(p) for p in near[-1]], [share(n)] * 4, 0)
        near.append(exchange(parts, axis))
    total = call(
        total_kernel, 1, [whole(p) for p in near[2]], [whole(shape(width, cols, dtype=F32))] * 3, 0
    )
    early = lambda a: (0, jnp.minimum(a, 1))
    late = lambda a: (0, jnp.maximum(a - 2, 0))
    layer_out, = call(
        layer_kernel, 4,
        [whole(plain), (mixed0, (TILE, width), lambda a: (jnp.minimum(a, 1), 0)),
         (mixed1, (TILE, width), lambda a: (jnp.maximum(a - 2, 0), 0))]
        + [(b, (piece, TILE), early) for b in merged0] + [(b, (piece, TILE), late) for b in merged1],
        [rows_at(shape(rows, width), TILE)], 2 * rows * width * width,
    )
    grad_input, = call(
        last_kernel, 4,
        [whole(got), whole(fac_inner), (base0, (inner, width), lambda a: (jnp.minimum(a, 1), 0)),
         (base1, (inner, width), lambda a: (jnp.maximum(a - 2, 0), 0))],
        [rows_at(shape(rows, width), inner)], inner_flops, (pltpu.VMEM((rows, width), BF),),
        after=(grad_kernel,),
    )
    return (layer_out, grad_input, grad_kernel, *total)


def solution(mesh):
    fine = Mesh(mesh.devices.reshape(4, 4, 4, 2, 2), CTX + TP)
    tok = P(CTX, TP)
    mat = P(TP, None)
    small = P(TP, CTX)
    freq = P(None, CTX, TP)
    return jax.shard_map(
        local,
        mesh=fine,
        in_specs=(tok, P(), P(), P(), P(), freq, mat, mat, mat, tok),
        out_specs=(tok, tok, freq, small, small, small),
        check_vma=False,
    )
```

```python
import functools
import math

import jax
import jax.numpy as jnp
from jax import lax
from jax.experimental import pallas as pl
from jax.experimental.pallas import tpu as pltpu
from jax.sharding import Mesh
from jax.sharding import PartitionSpec as P

CTX = ("y", "x", "z_lo")
TP = ("z_hi", "core")
HALVES = 2
BF = jnp.bfloat16
F32 = jnp.float32
TILE = 512
VMEM_LIMIT = 64 * 1024 * 1024
ROOT_HALF = math.sqrt(0.5)
INV_ROOT_2PI = 1.0 / math.sqrt(2.0 * math.pi)


def dot(left, right, dims=((1,), (0,)), precision=None):
    return lax.dot_general(
        left, right, (dims, ((), ())), precision=precision, preferred_element_type=F32
    )


def whole(array):
    return array, array.shape, lambda g: (0,) * len(array.shape)


def rows_at(array, n, start=0):
    return array, (n,) + array.shape[1:], lambda g: (start + g,) + (0,) * (len(array.shape) - 1)


def columns_at(array, n):
    return array, (array.shape[0], n), lambda g: (0, g)


def call(body, steps, args, outs, flops, scratch=(), after=()):
    arrays = [a[0] for a in args]
    n, late = len(args), len(after)

    def wrapped(*refs):
        body(*refs[:n], *refs[n + late :])

    moved = sum(math.prod(a.shape) * jnp.dtype(a.dtype).itemsize for a in arrays + [o[0] for o in outs])
    return pl.pallas_call(
        wrapped,
        grid=(steps,),
        out_shape=[o[0] for o in outs],
        in_specs=[pl.BlockSpec(a[1], a[2]) for a in args] + [pl.BlockSpec(memory_space=pl.ANY)] * late,
        out_specs=[pl.BlockSpec(o[1], o[2]) for o in outs],
        scratch_shapes=list(scratch),
        compiler_params=pltpu.CompilerParams(vmem_limit_bytes=VMEM_LIMIT),
        cost_estimate=pl.CostEstimate(
            flops=int(flops), bytes_accessed=int(moved), transcendentals=0
        ),
    )(*arrays, *after)


def interleave(parts):
    n, w = parts[0].shape
    cut = [p.reshape(n // 8, 1, 8, w) for p in parts]
    return jnp.concatenate(cut, axis=1).reshape(len(parts) * n, w).astype(BF)


def separate(rows, k):
    n, w = rows.shape
    cut = rows.astype(F32).reshape(n // (8 * k), k, 8, w)
    return [cut[:, i].reshape(n // k, w).astype(BF) for i in range(k)]


def inner_kernel(x_ref, mat_ref, out_ref):
    n = mat_ref.shape[0]
    part = mat_ref[...]
    blocks = [x_ref[i * n : (i + 1) * n, :] for i in range(x_ref.shape[0] // n)]
    out_ref[...] = interleave([dot(part, x, ((0,), (0,))) for x in blocks])


def widen(got_ref, wide):
    for c in range(wide.shape[0]):
        wide[c] = got_ref[:, c * 128 : (c + 1) * 128].astype(F32)


def rows_of(wide, e):
    parts, n, _ = wide.shape
    return jnp.concatenate(
        [wide[c, pl.ds(e, n // 8, stride=8), :].astype(BF) for c in range(parts)], axis=1
    )


def regroup_kernel(got_ref, out_ref, wide):
    widen(got_ref, wide)
    for e in range(8):
        out_ref[e] = rows_of(wide, e)


def spread(values, e, wide):
    parts, n, _ = wide.shape
    for c in range(parts):
        wide[c, pl.ds(e, n // 8, stride=8), :] = values[:, c * 128 : (c + 1) * 128]


def narrow(wide, out_ref):
    for c in range(wide.shape[0]):
        out_ref[:, c * 128 : (c + 1) * 128] = wide[c].astype(BF)


def there_kernel(got_ref, a_ref, b_ref, freq_ref, spec_ref, out0_ref, out1_ref, wide, back0, back1):
    step, each = pl.program_id(0), freq_ref.shape[0]

    @pl.when(step == 0)
    def _():
        widen(got_ref, wide)

    m = b_ref.shape[0] // 2
    for j in range(each):
        e = step * each + j
        values = dot(a_ref[...], rows_of(wide, e))
        spec_ref[j] = values
        result = dot(b_ref[...], (values * freq_ref[j].astype(F32)).astype(BF))
        spread(result[:m], e, back0)
        spread(result[m:], e, back1)

    @pl.when(step == 8 // each - 1)
    def _():
        narrow(back0, out0_ref)
        narrow(back1, out1_ref)


def back_kernel(first_ref, got_ref, a_ref, b_ref, freq_ref, spec_ref, grad_ref, out_ref, wide, back):
    step, each = pl.program_id(0), freq_ref.shape[0]

    @pl.when(step == 0)
    def _():
        widen(got_ref, wide)

    m = a_ref.shape[1] // 2
    for j in range(each):
        e = step * each + j
        values = dot(a_ref[:, :m], first_ref[j]) + dot(a_ref[:, m:], rows_of(wide, e))
        grad_ref[j] = values * spec_ref[j]
        spread(dot(b_ref[...], (values * freq_ref[j].astype(F32)).astype(BF)), e, back)

    @pl.when(step == 8 // each - 1)
    def _():
        narrow(back, out_ref)


def front_kernel(got_ref, mat_ref, x_ref, gate_w_ref, first_t_ref,
                 conv_ref, gate_ref, mixed_ref, s0_ref, s1_ref, s2_ref, s3_ref, parts):
    t = pl.program_id(0)
    n = mat_ref.shape[1]
    piece = s0_ref.shape[0]

    @pl.when(t == 0)
    def _():
        for i, part in enumerate(separate(got_ref[...], 2)):
            parts[i * n : (i + 1) * n, :] = part

    conv = dot(mat_ref[...], parts[pl.ds(pl.multiple_of(t * n, n), n), :])
    x = x_ref[...]
    gate = jax.nn.sigmoid(dot(x, gate_w_ref[...]))
    mixed = (x.astype(F32) + gate * conv).astype(BF)
    conv_ref[...] = conv
    gate_ref[...] = gate
    mixed_ref[...] = mixed
    first = dot(first_t_ref[...], mixed, ((1,), (1,))).astype(BF)
    for k, send in enumerate((s0_ref, s1_ref, s2_ref, s3_ref)):
        send[...] = first[k * piece : (k + 1) * piece, :]


def middle_kernel(*refs):
    shuf, up = refs[:4], refs[4:8]
    w_ref, wt_ref = refs[8:10]
    all_ref, gso_ref = refs[10:12]
    merged, back = refs[12:16], refs[16:20]
    piece = shuf[0].shape[0]
    xs = jnp.concatenate([r[...] for r in shuf], axis=0)
    ups = jnp.concatenate([r[...] for r in up], axis=0)
    all_ref[...] = xs
    out = dot(wt_ref[...], xs).astype(BF)
    m = out.astype(F32)
    slope = 0.5 * (1.0 + lax.erf(m * ROOT_HALF)) + m * (INV_ROOT_2PI * jnp.exp(-0.5 * m * m))
    gso = (ups.astype(F32) * slope).astype(BF)
    gso_ref[...] = gso
    gsh = dot(w_ref[...], gso).astype(BF)
    for k in range(4):
        merged[k][...] = out[k * piece : (k + 1) * piece, :]
        back[k][...] = gsh[k * piece : (k + 1) * piece, :]


def rear_kernel(g0_ref, g1_ref, g2_ref, g3_ref, first_t_ref, up_ref, gate_ref, conv_ref, mat_ref,
                gate_w_ref, out_ref, base_ref, ggp_ref, gfo_ref, opened_all):
    step = pl.program_id(0)
    n = mat_ref.shape[0]
    rows = up_ref.shape[0]
    gfo = jnp.concatenate([r[...] for r in (g0_ref, g1_ref, g2_ref, g3_ref)], axis=0)
    gfo_ref[...] = gfo
    gm = up_ref[...].astype(F32) + dot(gfo, first_t_ref[...], ((0,), (0,)))
    gate = gate_ref[...]
    opened = gm * gate
    opened_all[pl.ds(pl.multiple_of(step * rows, rows), rows), :] = opened.astype(BF)
    ggp = (opened * conv_ref[...] * (1.0 - gate)).astype(BF)
    ggp_ref[...] = ggp
    base_ref[...] = gm + dot(ggp, gate_w_ref[...], ((1,), (1,)))

    @pl.when(step == 2 * n // rows - 1)
    def _():
        for t in range(0, n, 256):
            part = mat_ref[t : t + 256, :]
            out_ref[2 * t : 2 * (t + 256), :] = interleave(
                [dot(part, opened_all[i * n : (i + 1) * n, :]) for i in range(2)]
            )


def layer_kernel(*refs):
    plain_ref, mixed, blocks, out_ref = refs[0], refs[1:3], (refs[3:7], refs[7:11]), refs[11]
    for i in range(2):

        @pl.when(pl.program_id(0) // 2 == i)
        def _(i=i):
            merged = jnp.concatenate([r[...] for r in blocks[i]], axis=0)
            m = dot(merged, plain_ref[...], ((0,), (0,)))
            gelu = 0.5 * m * (1.0 + lax.erf(m * ROOT_HALF))
            out_ref[...] = (mixed[i][...].astype(F32) + gelu).astype(BF)


def last_kernel(got_ref, mat_ref, base0_ref, base1_ref, out_ref, parts):
    a = pl.program_id(0)
    n = mat_ref.shape[0]

    @pl.when(a == 0)
    def _():
        for i, part in enumerate(separate(got_ref[...], 4)):
            parts[i * n : (i + 1) * n, :] = part

    conv_back = dot(mat_ref[...], parts[pl.ds(pl.multiple_of(a * n, n), n), :])

    @pl.when(a < 2)
    def _():
        out_ref[...] = (base0_ref[...] + conv_back).astype(BF)

    @pl.when(a >= 2)
    def _():
        out_ref[...] = (base1_ref[...] + conv_back).astype(BF)


def turn_kernel(x_ref, plain_ref, *sends):
    piece = sends[0].shape[0]
    turned = dot(plain_ref[...], x_ref[...], ((1,), (1,))).astype(BF)
    for k in range(4):
        sends[k][...] = turned[k * piece : (k + 1) * piece, :]


def prepare_kernel(order_ref, io_ref, plain_ref, block_ref, mix1_ref, mix2_ref,
                   io_out, io_t_out, first_t_out, second_out, second_t_out):
    order = order_ref[...]
    io = dot(io_ref[...], order, ((1,), (1,)))
    io_out[...] = io.astype(BF)
    io_t_out[...] = io.T.astype(BF)
    first_t_out[...] = dot(plain_ref[...], mix1_ref[...], ((1,), (1,))).astype(BF)
    block = block_ref[...]
    second = dot(dot(block, mix2_ref[...]).astype(BF), block, ((1,), (1,)))
    second_out[...] = second.astype(BF)
    second_t_out[...] = second.T.astype(BF)


def thirds(x):
    high = x.astype(BF)
    rest = x - high.astype(F32)
    middle = rest.astype(BF)
    return high, middle, (rest - middle.astype(F32)).astype(BF)


def pack_kernel(s0_ref, s1_ref, s2_ref, pick_ref, pick_plain_ref, pick_block_ref, block_ref,
                *outs, scale):
    s2 = sum(dot(p, block_ref[...]) for p in thirds(s2_ref[...]))
    cut = [thirds(s0_ref[...]), thirds(s1_ref[...]), thirds(s2)]
    w = s0_ref.shape[1]
    n = pick_ref.shape[0] // 4
    for k in range(4):
        parts = [
            (sum(dot(p[k * n : (k + 1) * n, :], x) for x in c) * scale).reshape(n // 8, 8, w)
            for p, c in zip((pick_ref, pick_plain_ref, pick_block_ref), cut)
        ]
        outs[k][...] = jnp.concatenate(parts, axis=1).reshape(3 * n, w).astype(outs[k].dtype)


def add_kernel(a_ref, b_ref, c_ref, d_ref, *outs):
    n = outs[0].shape[0]
    for k, out in enumerate(outs):
        at = slice(k * n, (k + 1) * n)
        a, b, c, d = (r[at, :].astype(F32) for r in (a_ref, b_ref, c_ref, d_ref))
        out[...] = (a + b) + (c + d)


def total_kernel(a_ref, b_ref, c_ref, d_ref, *outs):
    total = (a_ref[...] + b_ref[...]) + (c_ref[...] + d_ref[...])
    for i, out in enumerate(outs):
        out[...] = total[8 * i : 8 * i + out.shape[0]]


def swap(x):
    return lax.all_to_all(x, CTX, 0, 0, tiled=True)


def exchange(blocks, axes=TP):
    return [blocks[0]] + [
        lax.ppermute(blocks[k], axes, [(i, i ^ k) for i in range(4)]) for k in (1, 2, 3)
    ]


def one_hot(rows, columns, match):
    r = lax.broadcasted_iota(jnp.int32, (rows, columns), 0)
    c = lax.broadcasted_iota(jnp.int32, (rows, columns), 1)
    return match(r, c)


def local(
    hidden_in, fac_inner, fac_outer, inv_outer, inv_inner,
    kernel_freq, gate_blocks, mix_first, mix_second, upstream,
):
    rows, width = hidden_in.shape
    inner, outer = fac_inner.shape[0], fac_outer.shape[0]
    ctx = outer // (rows // inner)
    piece = width // 4
    toks = rows // HALVES
    cols = width // ctx
    me = lax.axis_index(TP)
    pair = range(HALVES)

    def shape(*dims, dtype=BF):
        return jax.ShapeDtypeStruct(dims, dtype)

    tall = [columns_at(shape(piece, toks), TILE)] * 4
    sheet = shape(toks, width)
    wide_sheet = shape(toks, width, dtype=F32)
    tiles = toks // TILE

    def plain_of(r):
        return ((r // piece) ^ me) * piece + r % piece

    def block_of(r):
        return (r % piece) * 4 + ((r // piece) ^ me)

    def outer_of(r):
        return (r % (2 * ctx)) // 2 * 4 + r // (2 * ctx) * 2 + r % 2

    def share_of(r):
        near = r // 8
        at = (((near // 16) ^ lax.axis_index("y")) * 4 + ((near // 4 % 4) ^ lax.axis_index("x"))) * 4
        at = at + ((near % 4) ^ lax.axis_index("z_lo"))
        return jnp.where(r % 8 < cols, at * cols + r % 8, -1)

    plain = one_hot(width, width, lambda r, c: plain_of(r) == c).astype(BF)
    block = one_hot(width, width, lambda r, c: block_of(r) == c).astype(BF)
    order = one_hot(outer, outer, lambda r, c: outer_of(r) == c).astype(BF)
    pick = one_hot(ctx * 8, width, lambda r, c: share_of(r) == c).astype(BF)
    pick_plain = one_hot(ctx * 8, width, lambda r, c: share_of(r) == plain_of(c)).astype(BF)
    pick_block = one_hot(ctx * 8, width, lambda r, c: share_of(r) == block_of(c)).astype(BF)

    inner_flops = 2 * rows * width * inner
    sent = call(
        inner_kernel, 2, [whole(hidden_in), columns_at(fac_inner, inner // 2)],
        [rows_at(shape(rows, width), rows // 2)], inner_flops,
    )
    got = swap(sent[0])
    up = [
        exchange(call(
            turn_kernel, tiles, [rows_at(upstream, TILE, i * tiles), whole(plain)], tall,
            2 * toks * width * width, after=sent,
        ))
        for i in pair
    ]
    square = whole(shape(width, width))
    io, io_t, first_t, second, second_t = call(
        prepare_kernel, 1, [whole(m) for m in (order, inv_outer, plain, block, mix_first, mix_second)],
        [whole(shape(outer, outer))] * 2 + [square] * 3, 4 * outer**3 + 6 * width**3, after=sent,
    )
    freq = kernel_freq.transpose(1, 0, 2)
    inv_inner_t = inv_inner.T

    half = outer // 2
    eb = 8
    wide = pltpu.VMEM((width // 128, rows, 128), F32)
    thin = pltpu.VMEM((width // 128, toks, 128), F32)
    spec_flops = 2 * 2 * outer * outer * eb * width
    spectrum, *sent = call(
        there_kernel, 2, [whole(got), whole(fac_outer.T), whole(io_t), rows_at(freq, 4)],
        [rows_at(shape(eb, outer, width, dtype=F32), 4), whole(sheet), whole(sheet)],
        spec_flops, (wide, thin, thin),
        after=(*up[0][2:], up[1][2], first_t, second, second_t, inv_inner_t, pick, pick_plain, pick_block),
    )
    got = [swap(s) for s in sent]

    def front(i, after=()):
        return call(
            front_kernel, tiles,
            [whole(got[i]), whole(inv_inner_t), rows_at(hidden_in, TILE, i * tiles), whole(gate_blocks),
             whole(first_t)],
            [rows_at(wide_sheet, TILE), rows_at(wide_sheet, TILE), rows_at(sheet, TILE)] + tall,
            2 * toks * width * (inner + 2 * width), (pltpu.VMEM((toks, width), BF),), after,
        )

    def middle(i, shuf, after=()):
        return call(
            middle_kernel, tiles,
            [columns_at(b, TILE) for b in (*shuf, *up[i])] + [whole(second), whole(second_t)],
            [columns_at(shape(width, toks), TILE)] * 2 + tall * 2, 2 * toks * width * 2 * width,
            (), after,
        )

    def rear(i, back, gate, conv, after=()):
        return call(
            rear_kernel, tiles,
            [columns_at(b, TILE) for b in back]
            + [whole(first_t), rows_at(upstream, TILE, i * tiles), rows_at(gate, TILE),
               rows_at(conv, TILE), whole(inv_inner), whole(gate_blocks)],
            [whole(sheet), rows_at(wide_sheet, TILE), rows_at(sheet, TILE),
             columns_at(shape(width, toks), TILE)],
            2 * toks * width * (inner + 2 * width), (pltpu.VMEM((toks, width), BF),), after,
        )

    conv0, gate0, mixed0, *blocks = front(0)
    shuf0 = exchange(blocks)
    conv1, gate1, mixed1, *blocks = front(1, (shuf0[2],))
    shuf1 = exchange(blocks)
    all0, gso0, *blocks0 = middle(0, shuf0, (mixed1, shuf1[1]))
    back0 = exchange(blocks0[4:])
    all1, gso1, *blocks1 = middle(1, shuf1)
    back1 = exchange(blocks1[4:])
    sent0, base0, ggp0, gfo0 = rear(0, back0, gate0, conv0, (gso1,))
    got = [swap(sent0)]
    merged0 = exchange(blocks0[:4])
    merged1 = exchange(blocks1[:4])
    x0, x1 = hidden_in[:toks], hidden_in[toks:]
    gate_sum = dot(ggp0, x0, ((0,), (0,)))
    first_sum = dot(gfo0, mixed0)
    second_sum = dot(gso0, all0, ((1,), (1,))) + dot(gso1, all1, ((1,), (1,)))
    sent1, base1, ggp1, gfo1 = rear(1, back1, gate1, conv1, (gate_sum, first_sum, second_sum, *merged0[2:]))
    got.append(swap(sent1))
    sums = (
        gate_sum + dot(ggp1, x1, ((0,), (0,))),
        first_sum + dot(gfo1, mixed1),
        second_sum,
    )

    shares = ctx * 24
    near = []

    def share(n):
        return whole(shape(n, width, dtype=F32))

    parts = call(
        functools.partial(pack_kernel, scale=1.0 / math.sqrt(rows * ctx)), 1,
        [whole(m) for m in (*sums, pick, pick_plain, pick_block, block)], [share(shares // 4)] + [whole(shape(shares // 4, width))] * 3,
        18 * shares * width * width, after=tuple(merged0[2:]),
    )
    near.append(exchange(parts, "y"))

    first, = call(
        regroup_kernel, 1, [whole(got[0])], [whole(shape(eb, half, width))], 0, (thin,),
    )
    grad_kernel, sent = call(
        back_kernel, 2,
        [rows_at(first, 4), whole(got[1]), whole(io), whole(fac_outer), rows_at(freq, 4), rows_at(spectrum, 4)],
        [rows_at(shape(eb, outer, width, dtype=F32), 4), whole(shape(rows, width))],
        spec_flops, (thin, wide), after=(*near[0][1:], *merged1[2:]),
    )
    got = swap(sent)
    grad_kernel = grad_kernel.transpose(1, 0, 2)
    early = lambda a: (0, jnp.minimum(a, 1))
    late = lambda a: (0, jnp.maximum(a - 2, 0))
    layer_out, = call(
        layer_kernel, 4,
        [whole(plain), (mixed0, (TILE, width), lambda a: (jnp.minimum(a, 1), 0)),
         (mixed1, (TILE, width), lambda a: (jnp.maximum(a - 2, 0), 0))]
        + [(b, (piece, TILE), early) for b in merged0] + [(b, (piece, TILE), late) for b in merged1],
        [rows_at(shape(rows, width), TILE)], 2 * rows * width * width,
    )
    for axis, n, ahead in (("x", shares // 16, ()), ("z_lo", shares // 64, (grad_kernel, layer_out))):
        parts = call(add_kernel, 1, [whole(p) for p in near[-1]], [share(n)] * 4, 0, after=ahead)
        near.append(exchange(parts, axis))
    total = call(
        total_kernel, 1, [whole(p) for p in near[2]], [whole(shape(cols, width, dtype=F32))] * 3, 0
    )
    total = [t.T for t in total]
    grad_input, = call(
        last_kernel, 4,
        [whole(got), whole(fac_inner), (base0, (inner, width), lambda a: (jnp.minimum(a, 1), 0)),
         (base1, (inner, width), lambda a: (jnp.maximum(a - 2, 0), 0))],
        [rows_at(shape(rows, width), inner)], inner_flops, (pltpu.VMEM((rows, width), BF),),
        after=(grad_kernel,),
    )
    return (layer_out, grad_input, grad_kernel, *total)


def solution(mesh):
    fine = Mesh(mesh.devices.reshape(4, 4, 4, 2, 2), CTX + TP)
    tok = P(CTX, TP)
    mat = P(TP, None)
    small = P(TP, CTX)
    freq = P(None, CTX, TP)
    return jax.shard_map(
        local,
        mesh=fine,
        in_specs=(tok, P(), P(), P(), P(), freq, mat, mat, mat, tok),
        out_specs=(tok, tok, freq, small, small, small),
        check_vma=False,
    )
```

```python
import functools
import math

import jax
import jax.numpy as jnp
from jax import lax
from jax.experimental import pallas as pl
from jax.experimental.pallas import tpu as pltpu
from jax.sharding import Mesh
from jax.sharding import PartitionSpec as P

CTX = ("y", "x", "z_lo")
TP = ("z_hi", "core")
HALVES = 2
BF = jnp.bfloat16
F32 = jnp.float32
TILE = 512
VMEM_LIMIT = 64 * 1024 * 1024
ROOT_HALF = math.sqrt(0.5)
INV_ROOT_2PI = 1.0 / math.sqrt(2.0 * math.pi)


def dot(left, right, dims=((1,), (0,)), precision=None):
    return lax.dot_general(
        left, right, (dims, ((), ())), precision=precision, preferred_element_type=F32
    )


def whole(array):
    return array, array.shape, lambda g: (0,) * len(array.shape)


def rows_at(array, n, start=0):
    return array, (n,) + array.shape[1:], lambda g: (start + g,) + (0,) * (len(array.shape) - 1)


def columns_at(array, n):
    return array, (array.shape[0], n), lambda g: (0, g)


def call(body, steps, args, outs, flops, scratch=(), after=()):
    arrays = [a[0] for a in args]
    n, late = len(args), len(after)

    def wrapped(*refs):
        body(*refs[:n], *refs[n + late :])

    moved = sum(math.prod(a.shape) * jnp.dtype(a.dtype).itemsize for a in arrays + [o[0] for o in outs])
    return pl.pallas_call(
        wrapped,
        grid=(steps,),
        out_shape=[o[0] for o in outs],
        in_specs=[pl.BlockSpec(a[1], a[2]) for a in args] + [pl.BlockSpec(memory_space=pl.ANY)] * late,
        out_specs=[pl.BlockSpec(o[1], o[2]) for o in outs],
        scratch_shapes=list(scratch),
        compiler_params=pltpu.CompilerParams(vmem_limit_bytes=VMEM_LIMIT),
        cost_estimate=pl.CostEstimate(
            flops=int(flops), bytes_accessed=int(moved), transcendentals=0
        ),
    )(*arrays, *after)


def interleave(parts):
    n, w = parts[0].shape
    cut = [p.reshape(n // 8, 1, 8, w) for p in parts]
    return jnp.concatenate(cut, axis=1).reshape(len(parts) * n, w).astype(BF)


def separate(rows, k):
    n, w = rows.shape
    cut = rows.astype(F32).reshape(n // (8 * k), k, 8, w)
    return [cut[:, i].reshape(n // k, w).astype(BF) for i in range(k)]


def inner_kernel(x_ref, mat_ref, out_ref):
    n = mat_ref.shape[0]
    part = mat_ref[...]
    blocks = [x_ref[i * n : (i + 1) * n, :] for i in range(x_ref.shape[0] // n)]
    out_ref[...] = interleave([dot(part, x, ((0,), (0,))) for x in blocks])


def widen(got_ref, wide):
    for c in range(wide.shape[0]):
        wide[c] = got_ref[:, c * 128 : (c + 1) * 128].astype(F32)


def rows_of(wide, e):
    parts, n, _ = wide.shape
    return jnp.concatenate(
        [wide[c, pl.ds(e, n // 8, stride=8), :].astype(BF) for c in range(parts)], axis=1
    )


def regroup_kernel(got_ref, out_ref, wide):
    widen(got_ref, wide)
    for e in range(8):
        out_ref[e] = rows_of(wide, e)


def spread(values, e, wide):
    parts, n, _ = wide.shape
    for c in range(parts):
        wide[c, pl.ds(e, n // 8, stride=8), :] = values[:, c * 128 : (c + 1) * 128]


def narrow(wide, out_ref):
    for c in range(wide.shape[0]):
        out_ref[:, c * 128 : (c + 1) * 128] = wide[c].astype(BF)


def there_kernel(got_ref, a_ref, b_ref, freq_ref, spec_ref, out0_ref, out1_ref, wide, back0, back1):
    step, each = pl.program_id(0), freq_ref.shape[0]

    @pl.when(step == 0)
    def _():
        widen(got_ref, wide)

    m = b_ref.shape[0] // 2
    for j in range(each):
        e = step * each + j
        values = dot(a_ref[...], rows_of(wide, e))
        spec_ref[j] = values
        result = dot(b_ref[...], (values * freq_ref[j].astype(F32)).astype(BF))
        spread(result[:m], e, back0)
        spread(result[m:], e, back1)

    @pl.when(step == 8 // each - 1)
    def _():
        narrow(back0, out0_ref)
        narrow(back1, out1_ref)


def back_kernel(first_ref, got_ref, a_ref, b_ref, freq_ref, spec_ref, grad_ref, out_ref, wide, back):
    step, each = pl.program_id(0), freq_ref.shape[0]

    @pl.when(step == 0)
    def _():
        widen(got_ref, wide)

    m = a_ref.shape[1] // 2
    for j in range(each):
        e = step * each + j
        values = dot(a_ref[:, :m], first_ref[j]) + dot(a_ref[:, m:], rows_of(wide, e))
        grad_ref[j] = values * spec_ref[j]
        spread(dot(b_ref[...], (values * freq_ref[j].astype(F32)).astype(BF)), e, back)

    @pl.when(step == 8 // each - 1)
    def _():
        narrow(back, out_ref)


def front_kernel(got_ref, mat_ref, x_ref, gate_w_ref, first_t_ref,
                 conv_ref, gate_ref, mixed_ref, s0_ref, s1_ref, s2_ref, s3_ref, parts):
    t = pl.program_id(0)
    n = mat_ref.shape[1]
    piece = s0_ref.shape[0]

    @pl.when(t == 0)
    def _():
        for i, part in enumerate(separate(got_ref[...], 2)):
            parts[i * n : (i + 1) * n, :] = part

    conv = dot(mat_ref[...], parts[pl.ds(pl.multiple_of(t * n, n), n), :])
    x = x_ref[...]
    gate = jax.nn.sigmoid(dot(x, gate_w_ref[...]))
    mixed = (x.astype(F32) + gate * conv).astype(BF)
    conv_ref[...] = conv
    gate_ref[...] = gate
    mixed_ref[...] = mixed
    first = dot(first_t_ref[...], mixed, ((1,), (1,))).astype(BF)
    for k, send in enumerate((s0_ref, s1_ref, s2_ref, s3_ref)):
        send[...] = first[k * piece : (k + 1) * piece, :]


def middle_kernel(*refs):
    shuf, up = refs[:4], refs[4:8]
    w_ref, wt_ref = refs[8:10]
    all_ref, gso_ref = refs[10:12]
    merged, back = refs[12:16], refs[16:20]
    piece = shuf[0].shape[0]
    xs = jnp.concatenate([r[...] for r in shuf], axis=0)
    ups = jnp.concatenate([r[...] for r in up], axis=0)
    all_ref[...] = xs
    out = dot(wt_ref[...], xs).astype(BF)
    m = out.astype(F32)
    slope = 0.5 * (1.0 + lax.erf(m * ROOT_HALF)) + m * (INV_ROOT_2PI * jnp.exp(-0.5 * m * m))
    gso = (ups.astype(F32) * slope).astype(BF)
    gso_ref[...] = gso
    gsh = dot(w_ref[...], gso).astype(BF)
    for k in range(4):
        merged[k][...] = out[k * piece : (k + 1) * piece, :]
        back[k][...] = gsh[k * piece : (k + 1) * piece, :]


def rear_kernel(g0_ref, g1_ref, g2_ref, g3_ref, first_t_ref, up_ref, gate_ref, conv_ref, mat_ref,
                gate_w_ref, out_ref, base_ref, ggp_ref, gfo_ref, opened_all):
    step = pl.program_id(0)
    n = mat_ref.shape[0]
    rows = up_ref.shape[0]
    gfo = jnp.concatenate([r[...] for r in (g0_ref, g1_ref, g2_ref, g3_ref)], axis=0)
    gfo_ref[...] = gfo
    gm = up_ref[...].astype(F32) + dot(gfo, first_t_ref[...], ((0,), (0,)))
    gate = gate_ref[...]
    opened = gm * gate
    opened_all[pl.ds(pl.multiple_of(step * rows, rows), rows), :] = opened.astype(BF)
    ggp = (opened * conv_ref[...] * (1.0 - gate)).astype(BF)
    ggp_ref[...] = ggp
    base_ref[...] = gm + dot(ggp, gate_w_ref[...], ((1,), (1,)))

    @pl.when(step == 2 * n // rows - 1)
    def _():
        for t in range(0, n, 256):
            part = mat_ref[t : t + 256, :]
            out_ref[2 * t : 2 * (t + 256), :] = interleave(
                [dot(part, opened_all[i * n : (i + 1) * n, :]) for i in range(2)]
            )


def layer_kernel(*refs):
    plain_ref, mixed, blocks, out_ref = refs[0], refs[1:3], (refs[3:7], refs[7:11]), refs[11]
    for i in range(2):

        @pl.when(pl.program_id(0) // 2 == i)
        def _(i=i):
            merged = jnp.concatenate([r[...] for r in blocks[i]], axis=0)
            m = dot(merged, plain_ref[...], ((0,), (0,)))
            gelu = 0.5 * m * (1.0 + lax.erf(m * ROOT_HALF))
            out_ref[...] = (mixed[i][...].astype(F32) + gelu).astype(BF)


def last_kernel(got_ref, mat_ref, base0_ref, base1_ref, out_ref, parts):
    a = pl.program_id(0)
    n = mat_ref.shape[0]

    @pl.when(a == 0)
    def _():
        for i, part in enumerate(separate(got_ref[...], 4)):
            parts[i * n : (i + 1) * n, :] = part

    conv_back = dot(mat_ref[...], parts[pl.ds(pl.multiple_of(a * n, n), n), :])

    @pl.when(a < 2)
    def _():
        out_ref[...] = (base0_ref[...] + conv_back).astype(BF)

    @pl.when(a >= 2)
    def _():
        out_ref[...] = (base1_ref[...] + conv_back).astype(BF)


def turn_kernel(x_ref, plain_ref, *sends):
    piece = sends[0].shape[0]
    turned = dot(plain_ref[...], x_ref[...], ((1,), (1,))).astype(BF)
    for k in range(4):
        sends[k][...] = turned[k * piece : (k + 1) * piece, :]


def prepare_kernel(order_ref, io_ref, plain_ref, block_ref, mix1_ref, mix2_ref,
                   io_out, io_t_out, first_t_out, second_out, second_t_out):
    order = order_ref[...]
    io = dot(io_ref[...], order, ((1,), (1,)))
    io_out[...] = io.astype(BF)
    io_t_out[...] = io.T.astype(BF)
    first_t_out[...] = dot(plain_ref[...], mix1_ref[...], ((1,), (1,))).astype(BF)
    block = block_ref[...]
    second = dot(dot(block, mix2_ref[...]).astype(BF), block, ((1,), (1,)))
    second_out[...] = second.astype(BF)
    second_t_out[...] = second.T.astype(BF)


def thirds(x):
    high = x.astype(BF)
    rest = x - high.astype(F32)
    middle = rest.astype(BF)
    return high, middle, (rest - middle.astype(F32)).astype(BF)


def pack_kernel(s0_ref, s1_ref, s2_ref, pick_ref, pick_plain_ref, pick_block_ref, block_ref,
                *outs, scale):
    s2 = sum(dot(p, block_ref[...]) for p in thirds(s2_ref[...]))
    cut = [thirds(s0_ref[...]), thirds(s1_ref[...]), thirds(s2)]
    w = s0_ref.shape[1]
    n = pick_ref.shape[0] // 4
    for k in range(4):
        parts = [
            (sum(dot(p[k * n : (k + 1) * n, :], x) for x in c) * scale).reshape(n // 8, 8, w)
            for p, c in zip((pick_ref, pick_plain_ref, pick_block_ref), cut)
        ]
        outs[k][...] = jnp.concatenate(parts, axis=1).reshape(3 * n, w).astype(outs[k].dtype)


def add_kernel(a_ref, b_ref, c_ref, d_ref, *outs):
    n = outs[0].shape[0]
    for k, out in enumerate(outs):
        at = slice(k * n, (k + 1) * n)
        a, b, c, d = (r[at, :].astype(F32) for r in (a_ref, b_ref, c_ref, d_ref))
        out[...] = (a + b) + (c + d)


def total_kernel(a_ref, b_ref, c_ref, d_ref, *outs):
    total = (a_ref[...] + b_ref[...]) + (c_ref[...] + d_ref[...])
    for i, out in enumerate(outs):
        out[...] = total[8 * i : 8 * i + out.shape[0]]


def swap(x):
    return lax.all_to_all(x, CTX, 0, 0, tiled=True)


def exchange(blocks, axes=TP):
    return [blocks[0]] + [
        lax.ppermute(blocks[k], axes, [(i, i ^ k) for i in range(4)]) for k in (1, 2, 3)
    ]


def one_hot(rows, columns, match):
    r = lax.broadcasted_iota(jnp.int32, (rows, columns), 0)
    c = lax.broadcasted_iota(jnp.int32, (rows, columns), 1)
    return match(r, c)


def local(
    hidden_in, fac_inner, fac_outer, inv_outer, inv_inner,
    kernel_freq, gate_blocks, mix_first, mix_second, upstream,
):
    rows, width = hidden_in.shape
    inner, outer = fac_inner.shape[0], fac_outer.shape[0]
    ctx = outer // (rows // inner)
    piece = width // 4
    toks = rows // HALVES
    cols = width // ctx
    me = lax.axis_index(TP)
    pair = range(HALVES)

    def shape(*dims, dtype=BF):
        return jax.ShapeDtypeStruct(dims, dtype)

    tall = [columns_at(shape(piece, toks), TILE)] * 4
    sheet = shape(toks, width)
    wide_sheet = shape(toks, width, dtype=F32)
    tiles = toks // TILE

    def plain_of(r):
        return ((r // piece) ^ me) * piece + r % piece

    def block_of(r):
        return (r % piece) * 4 + ((r // piece) ^ me)

    def outer_of(r):
        return (r % (2 * ctx)) // 2 * 4 + r // (2 * ctx) * 2 + r % 2

    def share_of(r):
        near = r // 8
        at = (((near // 16) ^ lax.axis_index("y")) * 4 + ((near // 4 % 4) ^ lax.axis_index("x"))) * 4
        at = at + ((near % 4) ^ lax.axis_index("z_lo"))
        return jnp.where(r % 8 < cols, at * cols + r % 8, -1)

    plain = one_hot(width, width, lambda r, c: plain_of(r) == c).astype(BF)
    block = one_hot(width, width, lambda r, c: block_of(r) == c).astype(BF)
    order = one_hot(outer, outer, lambda r, c: outer_of(r) == c).astype(BF)
    pick = one_hot(ctx * 8, width, lambda r, c: share_of(r) == c).astype(BF)
    pick_plain = one_hot(ctx * 8, width, lambda r, c: share_of(r) == plain_of(c)).astype(BF)
    pick_block = one_hot(ctx * 8, width, lambda r, c: share_of(r) == block_of(c)).astype(BF)

    inner_flops = 2 * rows * width * inner
    sent = call(
        inner_kernel, 2, [whole(hidden_in), columns_at(fac_inner, inner // 2)],
        [rows_at(shape(rows, width), rows // 2)], inner_flops,
    )
    got = swap(sent[0])
    up = [
        exchange(call(
            turn_kernel, tiles, [rows_at(upstream, TILE, i * tiles), whole(plain)], tall,
            2 * toks * width * width, after=sent,
        ))
        for i in pair
    ]
    square = whole(shape(width, width))
    io, io_t, first_t, second, second_t = call(
        prepare_kernel, 1, [whole(m) for m in (order, inv_outer, plain, block, mix_first, mix_second)],
        [whole(shape(outer, outer))] * 2 + [square] * 3, 4 * outer**3 + 6 * width**3, after=sent,
    )
    freq = kernel_freq.transpose(1, 0, 2)
    inv_inner_t = inv_inner.T

    half = outer // 2
    eb = 8
    wide = pltpu.VMEM((width // 128, rows, 128), F32)
    thin = pltpu.VMEM((width // 128, toks, 128), F32)
    spec_flops = 2 * 2 * outer * outer * eb * width
    spectrum, *sent = call(
        there_kernel, 2, [whole(got), whole(fac_outer.T), whole(io_t), rows_at(freq, 4)],
        [rows_at(shape(eb, outer, width, dtype=F32), 4), whole(sheet), whole(sheet)],
        spec_flops, (wide, thin, thin),
        after=(*up[0][2:], up[1][2], first_t, second, second_t, inv_inner_t, pick, pick_plain, pick_block),
    )
    got = [swap(s) for s in sent]

    def front(i, after=()):
        return call(
            front_kernel, tiles,
            [whole(got[i]), whole(inv_inner_t), rows_at(hidden_in, TILE, i * tiles), whole(gate_blocks),
             whole(first_t)],
            [rows_at(wide_sheet, TILE), rows_at(wide_sheet, TILE), rows_at(sheet, TILE)] + tall,
            2 * toks * width * (inner + 2 * width), (pltpu.VMEM((toks, width), BF),), after,
        )

    def middle(i, shuf, after=()):
        return call(
            middle_kernel, tiles,
            [columns_at(b, TILE) for b in (*shuf, *up[i])] + [whole(second), whole(second_t)],
            [columns_at(shape(width, toks), TILE)] * 2 + tall * 2, 2 * toks * width * 2 * width,
            (), after,
        )

    def rear(i, back, gate, conv, after=()):
        return call(
            rear_kernel, tiles,
            [columns_at(b, TILE) for b in back]
            + [whole(first_t), rows_at(upstream, TILE, i * tiles), rows_at(gate, TILE),
               rows_at(conv, TILE), whole(inv_inner), whole(gate_blocks)],
            [whole(sheet), rows_at(wide_sheet, TILE), rows_at(sheet, TILE),
             columns_at(shape(width, toks), TILE)],
            2 * toks * width * (inner + 2 * width), (pltpu.VMEM((toks, width), BF),), after,
        )

    conv0, gate0, mixed0, *blocks = front(0)
    shuf0 = exchange(blocks)
    conv1, gate1, mixed1, *blocks = front(1, (shuf0[2],))
    shuf1 = exchange(blocks)
    all0, gso0, *blocks0 = middle(0, shuf0, (mixed1, shuf1[1]))
    back0 = exchange(blocks0[4:])
    all1, gso1, *blocks1 = middle(1, shuf1)
    back1 = exchange(blocks1[4:])
    sent0, base0, ggp0, gfo0 = rear(0, back0, gate0, conv0, (gso1,))
    got = [swap(sent0)]
    merged0 = exchange(blocks0[:4])
    merged1 = exchange(blocks1[:4])
    x0, x1 = hidden_in[:toks], hidden_in[toks:]
    gate_sum = dot(ggp0, x0, ((0,), (0,)))
    first_sum = dot(gfo0, mixed0)
    second_sum = dot(gso0, all0, ((1,), (1,))) + dot(gso1, all1, ((1,), (1,)))
    sent1, base1, ggp1, gfo1 = rear(1, back1, gate1, conv1, (gate_sum, first_sum, second_sum))
    got.append(swap(sent1))
    sums = (
        gate_sum + dot(ggp1, x1, ((0,), (0,))),
        first_sum + dot(gfo1, mixed1),
        second_sum,
    )

    shares = ctx * 24
    near = []

    def share(n):
        return whole(shape(n, width, dtype=F32))

    parts = call(
        functools.partial(pack_kernel, scale=1.0 / math.sqrt(rows * ctx)), 1,
        [whole(m) for m in (*sums, pick, pick_plain, pick_block, block)], [share(shares // 4)] * 4,
        18 * shares * width * width, after=tuple(merged0[2:]),
    )
    near.append(exchange(parts, "y"))

    first, = call(
        regroup_kernel, 1, [whole(got[0])], [whole(shape(eb, half, width))], 0, (thin,),
    )
    grad_kernel, sent = call(
        back_kernel, 2,
        [rows_at(first, 4), whole(got[1]), whole(io), whole(fac_outer), rows_at(freq, 4), rows_at(spectrum, 4)],
        [rows_at(shape(eb, outer, width, dtype=F32), 4), whole(shape(rows, width))],
        spec_flops, (thin, wide), after=(*near[0][1:], *merged1[2:]),
    )
    got = swap(sent)
    grad_kernel = grad_kernel.transpose(1, 0, 2)
    early = lambda a: (0, jnp.minimum(a, 1))
    late = lambda a: (0, jnp.maximum(a - 2, 0))
    layer_out, = call(
        layer_kernel, 4,
        [whole(plain), (mixed0, (TILE, width), lambda a: (jnp.minimum(a, 1), 0)),
         (mixed1, (TILE, width), lambda a: (jnp.maximum(a - 2, 0), 0))]
        + [(b, (piece, TILE), early) for b in merged0] + [(b, (piece, TILE), late) for b in merged1],
        [rows_at(shape(rows, width), TILE)], 2 * rows * width * width,
    )
    for axis, n, ahead in (("x", shares // 16, ()), ("z_lo", shares // 64, (grad_kernel, layer_out))):
        parts = call(add_kernel, 1, [whole(p) for p in near[-1]], [share(n)] * 4, 0, after=ahead)
        near.append(exchange(parts, axis))
    total = call(
        total_kernel, 1, [whole(p) for p in near[2]], [whole(shape(cols, width, dtype=F32))] * 3, 0
    )
    total = [t.T for t in total]
    grad_input, = call(
        last_kernel, 4,
        [whole(got), whole(fac_inner), (base0, (inner, width), lambda a: (jnp.minimum(a, 1), 0)),
         (base1, (inner, width), lambda a: (jnp.maximum(a - 2, 0), 0))],
        [rows_at(shape(rows, width), inner)], inner_flops, (pltpu.VMEM((rows, width), BF),),
        after=(grad_kernel,),
    )
    return (layer_out, grad_input, grad_kernel, *total)


def solution(mesh):
    fine = Mesh(mesh.devices.reshape(4, 4, 4, 2, 2), CTX + TP)
    tok = P(CTX, TP)
    mat = P(TP, None)
    small = P(TP, CTX)
    freq = P(None, CTX, TP)
    return jax.shard_map(
        local,
        mesh=fine,
        in_specs=(tok, P(), P(), P(), P(), freq, mat, mat, mat, tok),
        out_specs=(tok, tok, freq, small, small, small),
        check_vma=False,
    )
```
